32 devices in a mesh: ctx: 8 (over z, x), tp: 4 (over y, core).
Axes of the slice: x: 2, y: 2, z: 4, core: 2. Of those that a mesh axis runs over, the one named last changes fastest.
Arguments:
- queries: bfloat16 [1024, 2048], P('ctx', 'tp'), may hold values from -6 to 6
- key_rows: bfloat16 [1024, 512], P('ctx', 'tp'), may hold values from -6 to 6
- value_matrix: bfloat16 [1024, 512], P('ctx', 'tp'), may hold values from -6 to 6
- attention_out: bfloat16 [1024, 2048], P('ctx', 'tp'), may hold values from -6 to 6
- output_grad: bfloat16 [1024, 2048], P('ctx', 'tp'), may hold values from -6 to 6
- w_query: bfloat16 [2048, 2048], P(None, 'tp'), may hold values from -3 to 3
- key_weight: bfloat16 [2048, 512], P(None, 'tp'), may hold values from -3 to 3
- value_weight: bfloat16 [2048, 512], P(None, 'tp'), may hold values from -3 to 3
- span_pos: int32 [16], replicated, may hold values from 0 to 15, as said below
Outputs:
- input_grad: bfloat16 [1024, 2048], P('ctx', 'tp')
The draws below stay inside these ranges and needn't reach their ends.
Inputs may be any that keep to these rules, and one draw needn't show every extreme that they name: Device d of ctx stores spans 2d and 2d + 1; their positions span_pos[2d] and span_pos[2d + 1] add up to 15, in either order; every position appears once.
All inputs are finite; a program needn't handle non-finite values.
Results may differ from the reference program's by a relative error of at most 0.0056.
Values may be sent and summed in bfloat16 or wider, within the bound.
A program may use at most 64 MiB of HBM per device.

```python
import jax
import jax.numpy as jnp
from jax import lax

MODEL_WIDTH = 2048
QUERY_HEADS = 16
KEY_VALUE_HEADS = 4
HEAD_SIZE = 128
SPAN_TOKENS = 64
SPAN_COUNT = 16
TOKEN_COUNT = 1024


def draw_queries(key, part):
    key = jax.random.fold_in(key, 11)
    base_offset = jnp.clip(jax.random.normal(key, (SPAN_COUNT, SPAN_TOKENS, QUERY_HEADS, HEAD_SIZE), jnp.float32), -6.0, 6.0)
    return base_offset.reshape(TOKEN_COUNT, QUERY_HEADS * HEAD_SIZE).astype(jnp.bfloat16)


def draw_key_rows(key, part):
    key = jax.random.fold_in(key, 23)
    base_offset = jnp.clip(jax.random.normal(key, (SPAN_COUNT, SPAN_TOKENS, KEY_VALUE_HEADS, HEAD_SIZE), jnp.float32), -6.0, 6.0)
    return base_offset.reshape(TOKEN_COUNT, KEY_VALUE_HEADS * HEAD_SIZE).astype(jnp.bfloat16)


def draw_span_pos(key, part):
    key = jax.random.fold_in(key, 37)
    order_key, flip_key = jax.random.split(key)
    lower = jax.random.permutation(order_key, SPAN_COUNT // 2).astype(jnp.int32)
    upper = (SPAN_COUNT - 1 - lower).astype(jnp.int32)
    flips = jax.random.randint(flip_key, (SPAN_COUNT // 2,), 0, 2, jnp.int32)
    first = jnp.where(flips == 0, lower, upper)
    second = jnp.where(flips == 0, upper, lower)
    return jnp.stack((first, second), axis=1).reshape(SPAN_COUNT).astype(jnp.int32)


def level_of(rng, dims, cuts, low, high):
    loudness = 1.0
    for axis_at, shards_of in cuts:
        steps = jax.random.uniform(jax.random.fold_in(jax.random.fold_in(rng, 6), axis_at), (shards_of,), jnp.float32, low / len(cuts), high / len(cuts))
        loudness = loudness * jnp.repeat(jnp.exp(steps), dims[axis_at] // shards_of).reshape((-1,) + (1,) * (len(dims) - 1 - axis_at))
    return loudness


def centred(rng, extent, spread, bound, pieces=(), kind=jnp.bfloat16):
    result = jax.random.normal(rng, extent, jnp.float32) * spread
    if len(pieces) > 0:
        result = level_of(rng, extent, pieces, -0.22, 0.18) * result
    return jnp.clip(result, min=-bound, max=bound).astype(kind)


def setup_inputs(seed: int = 0) -> dict:
    keys = jax.random.split(jax.random.key(seed), 10)
    return {
        "queries": draw_queries(jax.random.fold_in(keys[9], 71), 0),
        "key_rows": draw_key_rows(jax.random.fold_in(keys[9], 71), 0),
        "value_matrix": centred(keys[2], (TOKEN_COUNT, KEY_VALUE_HEADS * HEAD_SIZE), 1.0, 6.0, ((0, 8), (1, 4))),
        "attention_out": centred(keys[3], (TOKEN_COUNT, QUERY_HEADS * HEAD_SIZE), 1.0, 6.0, ((0, 8), (1, 4))),
        "output_grad": centred(keys[4], (TOKEN_COUNT, QUERY_HEADS * HEAD_SIZE), 1.0, 6.0, ((0, 8), (1, 4))),
        "w_query": centred(keys[5], (MODEL_WIDTH, QUERY_HEADS * HEAD_SIZE), 0.5, 3.0, ((1, 4),)),
        "key_weight": centred(keys[6], (MODEL_WIDTH, KEY_VALUE_HEADS * HEAD_SIZE), 0.5, 3.0, ((1, 4),)),
        "value_weight": centred(keys[7], (MODEL_WIDTH, KEY_VALUE_HEADS * HEAD_SIZE), 0.5, 3.0, ((1, 4),)),
        "span_pos": draw_span_pos(jax.random.fold_in(keys[9], 71), 0),
    }


def head_backward(query, grad_rows, deltas, key_rows, value_matrix):
    group_width = QUERY_HEADS // KEY_VALUE_HEADS
    score_scale = HEAD_SIZE ** -0.5
    key_block = min(512, TOKEN_COUNT)
    rows_block = key_block * group_width
    block_total = TOKEN_COUNT // key_block
    key_offsets = jnp.arange(key_block, dtype=jnp.int32)
    row_pos = jnp.repeat(jnp.arange(TOKEN_COUNT, dtype=jnp.int32), group_width)

    def scores_of(block_row, block_col):
        q_block = lax.dynamic_slice_in_dim(query, block_row * rows_block, rows_block, 0)
        k_block = lax.dynamic_slice_in_dim(key_rows, block_col * key_block, key_block, 0)
        raw_scores = jnp.dot(q_block, k_block.T, preferred_element_type=jnp.float32) * score_scale
        q_pos = lax.dynamic_slice_in_dim(row_pos, block_row * rows_block, rows_block, 0)
        allowed = (block_col * key_block + key_offsets)[None, :] <= q_pos[:, None]
        return raw_scores, allowed

    def row_stats(block_row):
        def stats_step(block_col, running):
            run_max, run_sum = running
            block_col = block_col.astype(jnp.int32)
            raw_scores, allowed = scores_of(block_row, block_col)
            masked = jnp.where(allowed, raw_scores, -jnp.inf)
            new_max = jnp.maximum(run_max, jnp.max(masked, axis=1))
            run_sum = run_sum * jnp.exp(run_max - new_max) + jnp.sum(jnp.exp(masked - new_max[:, None]), axis=1)
            return new_max, run_sum

        start_stats = (jnp.full((rows_block,), -jnp.inf, jnp.float32), jnp.zeros((rows_block,), jnp.float32))
        run_max, run_sum = lax.fori_loop(0, block_row + 1, stats_step, start_stats)
        return run_max + jnp.log(run_sum)

    log_totals = lax.map(row_stats, jnp.arange(block_total, dtype=jnp.int32)).reshape(-1)

    def query_block(outer, block_row):
        q_block = lax.dynamic_slice_in_dim(query, block_row * rows_block, rows_block, 0)
        g_block = lax.dynamic_slice_in_dim(grad_rows, block_row * rows_block, rows_block, 0)
        lse_block = lax.dynamic_slice_in_dim(log_totals, block_row * rows_block, rows_block, 0)
        delta_block = lax.dynamic_slice_in_dim(deltas, block_row * rows_block, rows_block, 0)

        def grad_step(block_col, inner):
            query_acc, key_acc, value_acc = inner
            block_col = block_col.astype(jnp.int32)
            raw_scores, allowed = scores_of(block_row, block_col)
            weights = jnp.where(allowed, jnp.exp(raw_scores - lse_block[:, None]), 0.0)
            probs_low = weights.astype(jnp.bfloat16)
            k_block = lax.dynamic_slice_in_dim(key_rows, block_col * key_block, key_block, 0)
            v_block = lax.dynamic_slice_in_dim(value_matrix, block_col * key_block, key_block, 0)
            grad_probs = jnp.dot(g_block, v_block.T, preferred_element_type=jnp.float32)
            grad_scores = (weights * (grad_probs - delta_block[:, None])).astype(jnp.bfloat16)
            query_acc = query_acc + jnp.dot(grad_scores, k_block, preferred_element_type=jnp.float32) * score_scale
            part_key = jnp.dot(grad_scores.T, q_block, preferred_element_type=jnp.float32) * score_scale
            part_value = jnp.dot(probs_low.T, g_block, preferred_element_type=jnp.float32)
            first_row = block_col * key_block
            key_acc = lax.dynamic_update_slice_in_dim(key_acc, lax.dynamic_slice_in_dim(key_acc, first_row, key_block, 0) + part_key, first_row, 0)
            value_acc = lax.dynamic_update_slice_in_dim(value_acc, lax.dynamic_slice_in_dim(value_acc, first_row, key_block, 0) + part_value, first_row, 0)
            return query_acc, key_acc, value_acc

        start_rows = jnp.zeros((rows_block, HEAD_SIZE), jnp.float32)
        query_acc, key_acc, value_acc = lax.fori_loop(0, block_row + 1, grad_step, (start_rows, outer[0], outer[1]))
        return (key_acc, value_acc), query_acc

    zero_keys = jnp.zeros((TOKEN_COUNT, HEAD_SIZE), jnp.float32)
    (key_acc, value_acc), query_acc = lax.scan(query_block, (zero_keys, zero_keys), jnp.arange(block_total, dtype=jnp.int32))
    return query_acc.reshape(TOKEN_COUNT, group_width * HEAD_SIZE), key_acc, value_acc


def reference(queries, key_rows, value_matrix, attention_out, output_grad, w_query, key_weight, value_weight, span_pos):
    group_width = QUERY_HEADS // KEY_VALUE_HEADS
    row_ids = jnp.arange(TOKEN_COUNT, dtype=jnp.int32)
    position = (span_pos[row_ids // SPAN_TOKENS] * SPAN_TOKENS + row_ids % SPAN_TOKENS).astype(jnp.int32)
    inverse = jnp.zeros((TOKEN_COUNT,), jnp.int32).at[position].set(row_ids)
    query_sorted = queries[inverse].reshape(TOKEN_COUNT, QUERY_HEADS, HEAD_SIZE)
    grad_sorted = output_grad[inverse].reshape(TOKEN_COUNT, QUERY_HEADS, HEAD_SIZE)
    key_sorted = key_rows[inverse]
    value_sorted = value_matrix[inverse]
    products = output_grad.astype(jnp.float32) * attention_out.astype(jnp.float32)
    delta_sorted = jnp.sum(products.reshape(TOKEN_COUNT, QUERY_HEADS, HEAD_SIZE), axis=2)[inverse]
    query_parts, key_parts, value_parts = [], [], []
    for head_number in range(KEY_VALUE_HEADS):
        low = head_number * group_width
        high = low + group_width
        query_head = query_sorted[:, low:high].reshape(TOKEN_COUNT * group_width, HEAD_SIZE)
        grad_head = grad_sorted[:, low:high].reshape(TOKEN_COUNT * group_width, HEAD_SIZE)
        delta_head = delta_sorted[:, low:high].reshape(TOKEN_COUNT * group_width)
        part_query, part_key, part_value = head_backward(query_head, grad_head, delta_head, key_sorted[:, head_number * HEAD_SIZE:(head_number + 1) * HEAD_SIZE], value_sorted[:, head_number * HEAD_SIZE:(head_number + 1) * HEAD_SIZE])
        query_parts.append(part_query)
        key_parts.append(part_key)
        value_parts.append(part_value)
    grad_query = jnp.concatenate(query_parts, axis=1)[position].astype(jnp.bfloat16)
    grad_key = jnp.concatenate(key_parts, axis=1)[position].astype(jnp.bfloat16)
    grad_value = jnp.concatenate(value_parts, axis=1)[position].astype(jnp.bfloat16)
    total = jnp.dot(grad_query, w_query.T, preferred_element_type=jnp.float32)
    total = total + jnp.dot(grad_key, key_weight.T, preferred_element_type=jnp.float32)
    total = total + jnp.dot(grad_value, value_weight.T, preferred_element_type=jnp.float32)
    return total.astype(jnp.bfloat16)
```

```python
import functools

import jax
import jax.numpy as jnp
from jax import lax
from jax.experimental import pallas as pl
from jax.experimental.pallas import tpu as pltpu
from jax.sharding import PartitionSpec as P

HEAD_SIZE = 128
PAIR = 2
SCORE_SCALE = HEAD_SIZE ** (-0.5)
LOG2_E = 1.4426950408889634
MESH = pl.DeviceIdType.MESH


def nt_dot(left, right):
    return lax.dot_general(
        left, right, (((1,), (1,)), ((), ())), preferred_element_type=jnp.float32
    )


def nn_dot(left, right):
    return lax.dot_general(
        left, right, (((1,), (0,)), ((), ())), preferred_element_type=jnp.float32
    )


def tn_dot(left, right):
    return lax.dot_general(
        left, right, (((0,), (0,)), ((), ())), preferred_element_type=jnp.float32
    )


def each(count, body):
    if count <= 8:
        for index in range(count):
            body(index)
    else:
        lax.fori_loop(0, count, lambda index, _: (body(index), 0)[1], 0)


def kernel(
    ctx_size,
    tp_size,
    q_ref,
    k_ref,
    v_ref,
    o_ref,
    g_ref,
    wq_ref,
    wk_ref,
    wv_ref,
    pos_ref,
    out_ref,
    q_in,
    g_in,
    o_in,
    wq,
    wk,
    wv,
    kv,
    q_rows,
    g_rows,
    delta,
    scores,
    row_max,
    row_sum,
    dq_t,
    pair_out,
    pair_in,
    own_part,
    far_out,
    far_in,
    proj,
    tp_out,
    tp_in,
    local_sem,
    kv_send,
    kv_fwd,
    kv_recv,
    pair_send,
    pair_recv,
    far_send,
    far_recv,
    tp_send,
    tp_recv,
):
    rows = q_ref.shape[0]
    span = rows // 2
    heads = q_ref.shape[1] // HEAD_SIZE
    query_rows = heads * rows
    far_size = ctx_size // PAIR
    features = out_ref.shape[1]
    chunk = min(far_size, 4)
    chunks = far_size // chunk
    chunk_rows = chunk * rows

    c = lax.axis_index("ctx")
    t = lax.axis_index("tp")
    a = lax.div(c, PAIR)
    b = lax.rem(c, PAIR)
    partner = (a * PAIR + 1 - b, t)

    def far(step):
        return lax.rem(a + step, far_size)

    def far_device(other):
        return (other * PAIR + b, t)

    local_pairs = [
        (q_ref, q_in),
        (g_ref, g_in),
        (o_ref, o_in),
        (k_ref, kv.at[0, b, a]),
        (v_ref, kv.at[1, b, a]),
        (wq_ref, wq),
        (wk_ref, wk),
        (wv_ref, wv),
    ]
    local_copies = [
        pltpu.make_async_copy(src, dst, local_sem.at[i]) for i, (src, dst) in enumerate(local_pairs)
    ]
    for copy in local_copies:
        copy.start()

    barrier = pltpu.get_barrier_semaphore()

    def greet_far(i):
        pl.semaphore_signal(barrier, inc=1, device_id=far_device(far(i + 1)), device_id_type=MESH)

    each(far_size - 1, greet_far)
    pl.semaphore_signal(barrier, inc=1, device_id=partner, device_id_type=MESH)
    for step in range(1, tp_size):
        pl.semaphore_signal(
            barrier, inc=1, device_id=(c, lax.rem(t + step, tp_size)), device_id_type=MESH
        )
    pl.semaphore_wait(barrier, far_size - 1 + 1 + tp_size - 1)

    def direct_copy(kind, i):
        return pltpu.make_async_remote_copy(
            src_ref=(k_ref, v_ref)[kind],
            dst_ref=kv.at[kind, b, a],
            send_sem=kv_send.at[kind, i],
            recv_sem=kv_recv.at[kind, b, a],
            device_id=far_device(far(i + 1)),
            device_id_type=MESH,
        )

    def own_forward(kind):
        return pltpu.make_async_remote_copy(
            src_ref=(k_ref, v_ref)[kind],
            dst_ref=kv.at[kind, b, a],
            send_sem=kv_fwd.at[kind, a],
            recv_sem=kv_recv.at[kind, b, a],
            device_id=partner,
            device_id_type=MESH,
        )

    def forward(kind, group, other):
        return pltpu.make_async_remote_copy(
            src_ref=kv.at[kind, group, other],
            dst_ref=kv.at[kind, group, other],
            send_sem=kv_fwd.at[kind, other],
            recv_sem=kv_recv.at[kind, group, other],
            device_id=partner,
            device_id_type=MESH,
        )

    for kind in range(2):
        each(far_size - 1, lambda i, kind=kind: direct_copy(kind, i).start())
        own_forward(kind).start()

    for copy in local_copies[:3]:
        copy.wait()
    for head in range(heads):
        lanes = slice(head * HEAD_SIZE, (head + 1) * HEAD_SIZE)
        held = slice(head * rows, (head + 1) * rows)
        q_rows[held, :] = q_in[:, lanes]
        g_head = g_in[:, lanes]
        g_rows[held, :] = g_head
        products = g_head.astype(jnp.float32) * o_in[:, lanes].astype(jnp.float32)
        delta[:, held] = jnp.sum(products.T, axis=0, keepdims=True)

    lane = lax.rem(lax.broadcasted_iota(jnp.int32, (1, query_rows), 1), rows)
    query_pos = lane + jnp.where(
        lane < span, pos_ref[PAIR * c] * span, pos_ref[PAIR * c + 1] * span - span
    )
    key_offset = lax.broadcasted_iota(jnp.int32, (span, 1), 0)

    row_max[...] = jnp.full_like(row_max, -jnp.inf)
    row_sum[...] = jnp.zeros_like(row_sum)
    dq_t[...] = jnp.zeros_like(dq_t)

    def block_start(index):
        return index * chunk_rows if isinstance(index, int) else pl.multiple_of(index * chunk_rows, chunk_rows)

    def score_chunk(which, group, index):
        first = index * chunk
        keys = kv[0, group, pl.ds(first, chunk)].reshape(chunk_rows, HEAD_SIZE)
        raw = nt_dot(keys, q_rows[...]) * (SCORE_SCALE * LOG2_E)
        best = row_max[...]
        for part in range(2 * chunk):
            stored = 2 * ((first + part // 2) * PAIR + group) + part % 2
            key_pos = pos_ref[stored] * span + key_offset
            masked = jnp.where(
                key_pos <= query_pos, raw[part * span : (part + 1) * span], -jnp.inf
            )
            scores[which, pl.ds(block_start(index) + part * span, span), :] = masked
            best = jnp.maximum(best, jnp.max(masked, axis=0, keepdims=True))
        row_max[...] = best

    def exp_chunk(which, index):
        at = pl.ds(block_start(index), chunk_rows)
        weights = jnp.exp2(scores[which, at, :] - row_max[...])
        scores[which, at, :] = weights
        row_sum[...] += jnp.sum(weights, axis=0, keepdims=True)

    def grad_chunk(which, group, index, inverse_sum):
        first = index * chunk
        keys = kv[0, group, pl.ds(first, chunk)].reshape(chunk_rows, HEAD_SIZE)
        values = kv[1, group, pl.ds(first, chunk)].reshape(chunk_rows, HEAD_SIZE)
        probs = scores[which, pl.ds(block_start(index), chunk_rows), :] * inverse_sum
        grad_probs = nt_dot(values, g_rows[...])
        grad_scores = (probs * (grad_probs - delta[...])).astype(jnp.bfloat16)
        part_value = nn_dot(probs.astype(jnp.bfloat16), g_rows[...])
        part_key = nn_dot(grad_scores, q_rows[...]) * SCORE_SCALE
        dq_t[...] += tn_dot(keys, grad_scores)
        target = pair_out if which == 1 else own_part
        target[pl.ds(first, chunk), 0] = part_key.reshape(chunk, rows, HEAD_SIZE).astype(target.dtype)
        target[pl.ds(first, chunk), 1] = part_value.reshape(chunk, rows, HEAD_SIZE).astype(target.dtype)

    def pass_on(kind):
        def one(i):
            other = far(i + 1)
            forward(kind, b, other).wait_recv()
            forward(kind, b, other).start()

        each(far_size - 1, one)

    def await_pair(kind):
        each(far_size, lambda i: forward(kind, 1 - b, i).wait_recv())

    pass_on(0)
    local_copies[3].wait()
    each(chunks, lambda i: score_chunk(0, b, i))
    pass_on(1)
    local_copies[4].wait()
    await_pair(0)
    each(chunks, lambda i: score_chunk(1, 1 - b, i))
    each(chunks, lambda i: exp_chunk(1, i))
    each(chunks, lambda i: exp_chunk(0, i))
    inverse_sum = 1.0 / row_sum[...]
    await_pair(1)
    each(chunks, lambda i: grad_chunk(1, 1 - b, i, inverse_sum))

    def pair_copy(other):
        return pltpu.make_async_remote_copy(
            src_ref=pair_out.at[other],
            dst_ref=pair_in.at[other],
            send_sem=pair_send.at[other],
            recv_sem=pair_recv.at[other],
            device_id=partner,
            device_id_type=MESH,
        )

    def far_copy(i):
        return pltpu.make_async_remote_copy(
            src_ref=far_out.at[i],
            dst_ref=far_in.at[i],
            send_sem=far_send.at[i],
            recv_sem=far_recv.at[i],
            device_id=far_device(far(i + 1)),
            device_id_type=MESH,
        )

    each(far_size, lambda i: pair_copy(far(i + 1)).start())
    each(chunks, lambda i: grad_chunk(0, b, i, inverse_sum))

    def send_far(i):
        other = far(i + 1)
        pair_copy(other).wait_recv()
        far_out[i] = (own_part[other] + pair_in[other].astype(jnp.float32)).astype(jnp.bfloat16)
        far_copy(i).start()

    each(far_size - 1, send_far)

    for copy in local_copies[5:]:
        copy.wait()
    grad_query = (dq_t[...] * SCORE_SCALE).astype(jnp.bfloat16)
    stacked = jnp.concatenate(
        [grad_query[:, head * rows : (head + 1) * rows] for head in range(heads)], axis=0
    )
    proj[...] = nn_dot(wq[...], stacked)

    pair_copy(a).wait_recv()
    own_part[a] += pair_in[a].astype(jnp.float32)

    def add_far(i):
        far_copy(i).wait_recv()
        own_part[a] += far_in[i].astype(jnp.float32)

    each(far_size - 1, add_far)
    grad_key = own_part[a, 0].astype(jnp.bfloat16)
    grad_value = own_part[a, 1].astype(jnp.bfloat16)

    def feature_block(owner):
        at = pl.ds(pl.multiple_of(owner * features, features), features)
        return proj[at, :] + nt_dot(wk[at, :], grad_key) + nt_dot(wv[at, :], grad_value)

    def tp_copy(step):
        return pltpu.make_async_remote_copy(
            src_ref=tp_out.at[step - 1],
            dst_ref=tp_in.at[step - 1],
            send_sem=tp_send.at[step - 1],
            recv_sem=tp_recv.at[step - 1],
            device_id=(c, lax.rem(t + step, tp_size)),
            device_id_type=MESH,
        )

    order = sorted(range(1, tp_size), key=lambda step: abs(step - tp_size // 2))
    for step in order:
        tp_out[step - 1] = feature_block(lax.rem(t + step, tp_size)).astype(jnp.bfloat16)
        tp_copy(step).start()
    total = feature_block(t)
    for step in reversed(order):
        tp_copy(step).wait_recv()
        total += tp_in[step - 1].astype(jnp.float32)
    out_ref[...] = total.T.astype(out_ref.dtype)

    for kind in range(2):
        each(far_size - 1, lambda i, kind=kind: direct_copy(kind, i).wait_send())
        each(far_size, lambda i, kind=kind: forward(kind, b, i).wait_send())
    each(far_size, lambda i: pair_copy(i).wait_send())
    each(far_size - 1, lambda i: far_copy(i).wait_send())
    for step in order:
        tp_copy(step).wait_send()


def local(ctx_size, tp_size, queries, key_rows, value_matrix, attention_out, output_grad, w_query, key_weight, value_weight, span_pos):
    rows, width = queries.shape
    model = w_query.shape[0]
    query_rows = rows * (width // HEAD_SIZE)
    far_size = ctx_size // PAIR
    features = model // tp_size
    block = (rows, HEAD_SIZE)
    low, full = jnp.bfloat16, jnp.float32
    dma = pltpu.SemaphoreType.DMA
    anywhere = pl.BlockSpec(memory_space=pl.ANY)
    return pl.pallas_call(
        functools.partial(kernel, ctx_size, tp_size),
        out_shape=jax.ShapeDtypeStruct((rows, features), low),
        in_specs=[anywhere] * 8 + [pl.BlockSpec(memory_space=pltpu.SMEM)],
        out_specs=pl.BlockSpec(memory_space=pltpu.VMEM),
        scratch_shapes=[
            pltpu.VMEM((rows, width), low),
            pltpu.VMEM((rows, width), low),
            pltpu.VMEM((rows, width), low),
            pltpu.VMEM(w_query.shape, low),
            pltpu.VMEM(key_weight.shape, low),
            pltpu.VMEM(value_weight.shape, low),
            pltpu.VMEM((2, PAIR, far_size) + block, low),
            pltpu.VMEM((query_rows, HEAD_SIZE), low),
            pltpu.VMEM((query_rows, HEAD_SIZE), low),
            pltpu.VMEM((1, query_rows), full),
            pltpu.VMEM((PAIR, far_size * rows, query_rows), full),
            pltpu.VMEM((1, query_rows), full),
            pltpu.VMEM((1, query_rows), full),
            pltpu.VMEM((HEAD_SIZE, query_rows), full),
            pltpu.VMEM((far_size, 2) + block, low),
            pltpu.VMEM((far_size, 2) + block, low),
            pltpu.VMEM((far_size, 2) + block, full),
            pltpu.VMEM((far_size - 1, 2) + block, low),
            pltpu.VMEM((far_size - 1, 2) + block, low),
            pltpu.VMEM((model, rows), full),
            pltpu.VMEM((tp_size - 1, features, rows), low),
            pltpu.VMEM((tp_size - 1, features, rows), low),
            dma((8,)),
            dma((2, far_size - 1)),
            dma((2, far_size)),
            dma((2, PAIR, far_size)),
            dma((far_size,)),
            dma((far_size,)),
            dma((far_size - 1,)),
            dma((far_size - 1,)),
            dma((tp_size - 1,)),
            dma((tp_size - 1,)),
        ],
        compiler_params=pltpu.CompilerParams(
            collective_id=0, has_side_effects=True, vmem_limit_bytes=52 * 1024 * 1024
        ),
    )(queries, key_rows, value_matrix, attention_out, output_grad, w_query, key_weight, value_weight, span_pos)


def solution(mesh):
    in_specs = (
        P("ctx", "tp"),
        P("ctx", "tp"),
        P("ctx", "tp"),
        P("ctx", "tp"),
        P("ctx", "tp"),
        P(None, "tp"),
        P(None, "tp"),
        P(None, "tp"),
        P(),
    )
    body = functools.partial(local, mesh.shape["ctx"], mesh.shape["tp"])
    return jax.shard_map(body, mesh=mesh, in_specs=in_specs, out_specs=P("ctx", "tp"), check_vma=False)
```

```python
import functools

import jax
import jax.numpy as jnp
from jax import lax
from jax.experimental import pallas as pl
from jax.experimental.pallas import tpu as pltpu
from jax.sharding import PartitionSpec as P

HEAD_SIZE = 128
PAIR = 2
SCORE_SCALE = HEAD_SIZE ** (-0.5)
LOG2_E = 1.4426950408889634
MESH = pl.DeviceIdType.MESH


def nt_dot(left, right):
    return lax.dot_general(
        left, right, (((1,), (1,)), ((), ())), preferred_element_type=jnp.float32
    )


def nn_dot(left, right):
    return lax.dot_general(
        left, right, (((1,), (0,)), ((), ())), preferred_element_type=jnp.float32
    )


def tn_dot(left, right):
    return lax.dot_general(
        left, right, (((0,), (0,)), ((), ())), preferred_element_type=jnp.float32
    )


def each(count, body):
    if count <= 8:
        for index in range(count):
            body(index)
    else:
        lax.fori_loop(0, count, lambda index, _: (body(index), 0)[1], 0)


def kernel(
    ctx_size,
    tp_size,
    q_ref,
    k_ref,
    v_ref,
    o_ref,
    g_ref,
    wq_ref,
    wk_ref,
    wv_ref,
    pos_ref,
    out_ref,
    q_in,
    g_in,
    o_in,
    wq,
    w_kv,
    kv,
    q_rows,
    g_rows,
    delta,
    scores,
    row_max,
    row_sum,
    dq_t,
    pair_out,
    pair_in,
    own_part,
    far_out,
    far_in,
    tp_out,
    tp_in,
    local_sem,
    kv_send,
    kv_fwd,
    kv_recv,
    pair_send,
    pair_recv,
    far_send,
    far_recv,
    tp_send,
    tp_recv,
    g_kv,
    w_send,
    w_recv,
    g_send,
    g_recv,
):
    rows = q_ref.shape[0]
    span = rows // 2
    heads = q_ref.shape[1] // HEAD_SIZE
    query_rows = heads * rows
    far_size = ctx_size // PAIR
    features = out_ref.shape[1]
    chunk = min(far_size, 4)
    chunks = far_size // chunk
    chunk_rows = chunk * rows

    c = lax.axis_index("ctx")
    t = lax.axis_index("tp")
    a = lax.div(c, PAIR)
    b = lax.rem(c, PAIR)
    partner = (a * PAIR + 1 - b, t)

    def far(step):
        return lax.rem(a + step, far_size)

    def far_device(other):
        return (other * PAIR + b, t)

    def feature_rows(owner):
        return pl.ds(pl.multiple_of(owner * features, features), features)

    def tp_peer(step):
        return lax.rem(t + step, tp_size)

    own_features = feature_rows(t)
    order = sorted(range(1, tp_size), key=lambda step: abs(step - tp_size // 2))

    local_pairs = [
        (q_ref, q_in),
        (g_ref, g_in),
        (o_ref, o_in),
        (k_ref, kv.at[0, b, a]),
        (v_ref, kv.at[1, b, a]),
        (wq_ref, wq),
        (wk_ref.at[own_features], w_kv.at[t, 0]),
        (wv_ref.at[own_features], w_kv.at[t, 1]),
    ]
    local_copies = [
        pltpu.make_async_copy(src, dst, local_sem.at[i]) for i, (src, dst) in enumerate(local_pairs)
    ]
    for copy in local_copies:
        copy.start()

    barrier = pltpu.get_barrier_semaphore()

    def greet_far(i):
        pl.semaphore_signal(barrier, inc=1, device_id=far_device(far(i + 1)), device_id_type=MESH)

    each(far_size - 1, greet_far)
    pl.semaphore_signal(barrier, inc=1, device_id=partner, device_id_type=MESH)
    for step in range(1, tp_size):
        pl.semaphore_signal(
            barrier, inc=1, device_id=(c, lax.rem(t + step, tp_size)), device_id_type=MESH
        )
    pl.semaphore_wait(barrier, far_size - 1 + 1 + tp_size - 1)

    def direct_copy(kind, i):
        return pltpu.make_async_remote_copy(
            src_ref=(k_ref, v_ref)[kind],
            dst_ref=kv.at[kind, b, a],
            send_sem=kv_send.at[kind, i],
            recv_sem=kv_recv.at[kind, b, a],
            device_id=far_device(far(i + 1)),
            device_id_type=MESH,
        )

    def own_forward(kind):
        return pltpu.make_async_remote_copy(
            src_ref=(k_ref, v_ref)[kind],
            dst_ref=kv.at[kind, b, a],
            send_sem=kv_fwd.at[kind, a],
            recv_sem=kv_recv.at[kind, b, a],
            device_id=partner,
            device_id_type=MESH,
        )

    def forward(kind, group, other):
        return pltpu.make_async_remote_copy(
            src_ref=kv.at[kind, group, other],
            dst_ref=kv.at[kind, group, other],
            send_sem=kv_fwd.at[kind, other],
            recv_sem=kv_recv.at[kind, group, other],
            device_id=partner,
            device_id_type=MESH,
        )

    for kind in range(2):
        each(far_size - 1, lambda i, kind=kind: direct_copy(kind, i).start())
        own_forward(kind).start()

    def weight_copy(step, kind):
        return pltpu.make_async_remote_copy(
            src_ref=(wk_ref, wv_ref)[kind].at[feature_rows(tp_peer(step))],
            dst_ref=w_kv.at[t, kind],
            send_sem=w_send.at[step - 1, kind],
            recv_sem=w_recv.at[step - 1, kind],
            device_id=(c, tp_peer(step)),
            device_id_type=MESH,
        )

    for kind in (1, 0):
        for step in order:
            weight_copy(step, kind).start()

    for copy in local_copies[:3]:
        copy.wait()
    for head in range(heads):
        lanes = slice(head * HEAD_SIZE, (head + 1) * HEAD_SIZE)
        held = slice(head * rows, (head + 1) * rows)
        q_rows[held, :] = q_in[:, lanes]
        g_head = g_in[:, lanes]
        g_rows[held, :] = g_head
        products = g_head.astype(jnp.float32) * o_in[:, lanes].astype(jnp.float32)
        delta[:, held] = jnp.sum(products.T, axis=0, keepdims=True)

    lane = lax.rem(lax.broadcasted_iota(jnp.int32, (1, query_rows), 1), rows)
    query_pos = lane + jnp.where(
        lane < span, pos_ref[PAIR * c] * span, pos_ref[PAIR * c + 1] * span - span
    )
    key_offset = lax.broadcasted_iota(jnp.int32, (span, 1), 0)

    row_max[...] = jnp.full_like(row_max, -jnp.inf)
    row_sum[...] = jnp.zeros_like(row_sum)
    dq_t[...] = jnp.zeros_like(dq_t)

    def block_start(index):
        return index * chunk_rows if isinstance(index, int) else pl.multiple_of(index * chunk_rows, chunk_rows)

    def score_chunk(which, group, index):
        first = index * chunk
        keys = kv[0, group, pl.ds(first, chunk)].reshape(chunk_rows, HEAD_SIZE)
        raw = nt_dot(keys, q_rows[...]) * (SCORE_SCALE * LOG2_E)
        best = row_max[...]
        for part in range(2 * chunk):
            stored = 2 * ((first + part // 2) * PAIR + group) + part % 2
            key_pos = pos_ref[stored] * span + key_offset
            masked = jnp.where(
                key_pos <= query_pos, raw[part * span : (part + 1) * span], -jnp.inf
            )
            scores[which, pl.ds(block_start(index) + part * span, span), :] = masked
            best = jnp.maximum(best, jnp.max(masked, axis=0, keepdims=True))
        row_max[...] = best

    def exp_chunk(which, index):
        at = pl.ds(block_start(index), chunk_rows)
        weights = jnp.exp2(scores[which, at, :] - row_max[...])
        scores[which, at, :] = weights
        row_sum[...] += jnp.sum(weights, axis=0, keepdims=True)

    def store_part(which, kind, first, part):
        target = pair_out if which == 1 else own_part
        target[kind, pl.ds(first, chunk)] = part.reshape(chunk, rows, HEAD_SIZE).astype(target.dtype)

    def value_chunk(which, index, inverse_sum):
        at = pl.ds(block_start(index), chunk_rows)
        probs = scores[which, at, :] * inverse_sum
        scores[which, at, :] = probs
        store_part(which, 1, index * chunk, nn_dot(probs.astype(jnp.bfloat16), g_rows[...]))

    def key_chunk(which, group, index):
        first = index * chunk
        keys = kv[0, group, pl.ds(first, chunk)].reshape(chunk_rows, HEAD_SIZE)
        values = kv[1, group, pl.ds(first, chunk)].reshape(chunk_rows, HEAD_SIZE)
        probs = scores[which, pl.ds(block_start(index), chunk_rows), :]
        grad_probs = nt_dot(values, g_rows[...])
        grad_scores = (probs * (grad_probs - delta[...])).astype(jnp.bfloat16)
        store_part(which, 0, first, nn_dot(grad_scores, q_rows[...]) * SCORE_SCALE)
        dq_t[...] += tn_dot(keys, grad_scores)

    def pass_on(kind):
        def one(i):
            other = far(i + 1)
            forward(kind, b, other).wait_recv()
            forward(kind, b, other).start()

        each(far_size - 1, one)

    def await_pair(kind):
        each(far_size, lambda i: forward(kind, 1 - b, i).wait_recv())

    pass_on(0)
    local_copies[3].wait()
    each(chunks, lambda i: score_chunk(0, b, i))
    pass_on(1)
    local_copies[4].wait()
    await_pair(0)
    each(chunks, lambda i: score_chunk(1, 1 - b, i))
    each(chunks, lambda i: exp_chunk(1, i))
    each(chunks, lambda i: exp_chunk(0, i))
    inverse_sum = 1.0 / row_sum[...]

    def pair_copy(kind, other):
        return pltpu.make_async_remote_copy(
            src_ref=pair_out.at[kind, other],
            dst_ref=pair_in.at[kind, other],
            send_sem=pair_send.at[kind, other],
            recv_sem=pair_recv.at[kind, other],
            device_id=partner,
            device_id_type=MESH,
        )

    def far_copy(kind, i):
        return pltpu.make_async_remote_copy(
            src_ref=far_out.at[kind, i],
            dst_ref=far_in.at[kind, i],
            send_sem=far_send.at[kind, i],
            recv_sem=far_recv.at[kind, i],
            device_id=far_device(far(i + 1)),
            device_id_type=MESH,
        )

    def send_far(kind, i):
        other = far(i + 1)
        pair_copy(kind, other).wait_recv()
        far_out[kind, i] = (
            own_part[kind, other] + pair_in[kind, other].astype(jnp.float32)
        ).astype(jnp.bfloat16)
        far_copy(kind, i).start()

    each(chunks, lambda i: value_chunk(1, i, inverse_sum))
    each(far_size, lambda i: pair_copy(1, far(i + 1)).start())
    each(chunks, lambda i: value_chunk(0, i, inverse_sum))
    await_pair(1)
    each(chunks, lambda i: key_chunk(1, 1 - b, i))
    each(far_size, lambda i: pair_copy(0, far(i + 1)).start())
    each(chunks, lambda i: key_chunk(0, b, i))
    each(far_size - 1, lambda i: send_far(1, i))

    local_copies[5].wait()
    grad_query = (dq_t[...] * SCORE_SCALE).astype(jnp.bfloat16)
    stacked = jnp.concatenate(
        [grad_query[:, head * rows : (head + 1) * rows] for head in range(heads)], axis=0
    )

    def tp_copy(step):
        return pltpu.make_async_remote_copy(
            src_ref=tp_out.at[step - 1],
            dst_ref=tp_in.at[step - 1],
            send_sem=tp_send.at[step - 1],
            recv_sem=tp_recv.at[step - 1],
            device_id=(c, tp_peer(step)),
            device_id_type=MESH,
        )

    for step in order:
        tp_out[step - 1] = nn_dot(wq[feature_rows(tp_peer(step)), :], stacked).astype(jnp.bfloat16)
        tp_copy(step).start()
    each(far_size - 1, lambda i: send_far(0, i))
    own_proj = nn_dot(wq[own_features, :], stacked)

    def grad_copy(step, kind):
        return pltpu.make_async_remote_copy(
            src_ref=g_kv.at[t, kind],
            dst_ref=g_kv.at[t, kind],
            send_sem=g_send.at[step - 1, kind],
            recv_sem=g_recv.at[step - 1, kind],
            device_id=(c, tp_peer(step)),
            device_id_type=MESH,
        )

    def add_far(kind, i):
        far_copy(kind, i).wait_recv()
        own_part[kind, a] += far_in[kind, i].astype(jnp.float32)

    def finish(kind):
        pair_copy(kind, a).wait_recv()
        own_part[kind, a] += pair_in[kind, a].astype(jnp.float32)
        each(far_size - 1, lambda i: add_far(kind, i))
        g_kv[t, kind] = own_part[kind, a].astype(jnp.bfloat16)
        for step in order:
            grad_copy(step, kind).start()

    finish(1)
    for step in reversed(order):
        tp_copy(step).wait_recv()
        own_proj += tp_in[step - 1].astype(jnp.float32)
    total = own_proj.T
    finish(0)
    for kind in (1, 0):
        local_copies[6 + kind].wait()
        total += nt_dot(g_kv[t, kind], w_kv[t, kind])
        for step in reversed(order):
            sender = lax.rem(t + tp_size - step, tp_size)
            weight_copy(step, kind).wait_recv()
            grad_copy(step, kind).wait_recv()
            total += nt_dot(g_kv[sender, kind], w_kv[sender, kind])
    out_ref[...] = total.astype(out_ref.dtype)

    for kind in range(2):
        each(far_size - 1, lambda i, kind=kind: direct_copy(kind, i).wait_send())
        each(far_size, lambda i, kind=kind: forward(kind, b, i).wait_send())
        each(far_size, lambda i, kind=kind: pair_copy(kind, i).wait_send())
        each(far_size - 1, lambda i, kind=kind: far_copy(kind, i).wait_send())
        for step in order:
            weight_copy(step, kind).wait_send()
            grad_copy(step, kind).wait_send()
    for step in order:
        tp_copy(step).wait_send()


def local(ctx_size, tp_size, queries, key_rows, value_matrix, attention_out, output_grad, w_query, key_weight, value_weight, span_pos):
    rows, width = queries.shape
    model = w_query.shape[0]
    query_rows = rows * (width // HEAD_SIZE)
    far_size = ctx_size // PAIR
    features = model // tp_size
    block = (rows, HEAD_SIZE)
    low, full = jnp.bfloat16, jnp.float32
    dma = pltpu.SemaphoreType.DMA
    in_hbm = pl.BlockSpec(memory_space=pltpu.HBM)
    return pl.pallas_call(
        functools.partial(kernel, ctx_size, tp_size),
        out_shape=jax.ShapeDtypeStruct((rows, features), low),
        in_specs=[in_hbm] * 8 + [pl.BlockSpec(memory_space=pltpu.SMEM)],
        out_specs=pl.BlockSpec(memory_space=pltpu.VMEM),
        scratch_shapes=[
            pltpu.VMEM((rows, width), low),
            pltpu.VMEM((rows, width), low),
            pltpu.VMEM((rows, width), low),
            pltpu.VMEM(w_query.shape, low),
            pltpu.VMEM((tp_size, 2, features, HEAD_SIZE), low),
            pltpu.VMEM((2, PAIR, far_size) + block, low),
            pltpu.VMEM((query_rows, HEAD_SIZE), low),
            pltpu.VMEM((query_rows, HEAD_SIZE), low),
            pltpu.VMEM((1, query_rows), full),
            pltpu.VMEM((PAIR, far_size * rows, query_rows), full),
            pltpu.VMEM((1, query_rows), full),
            pltpu.VMEM((1, query_rows), full),
            pltpu.VMEM((HEAD_SIZE, query_rows), full),
            pltpu.VMEM((2, far_size) + block, low),
            pltpu.VMEM((2, far_size) + block, low),
            pltpu.VMEM((2, far_size) + block, full),
            pltpu.VMEM((2, far_size - 1) + block, low),
            pltpu.VMEM((2, far_size - 1) + block, low),
            pltpu.VMEM((tp_size - 1, features, rows), low),
            pltpu.VMEM((tp_size - 1, features, rows), low),
            dma((8,)),
            dma((2, far_size - 1)),
            dma((2, far_size)),
            dma((2, PAIR, far_size)),
            dma((2, far_size)),
            dma((2, far_size)),
            dma((2, far_size - 1)),
            dma((2, far_size - 1)),
            dma((tp_size - 1,)),
            dma((tp_size - 1,)),
            pltpu.VMEM((tp_size, 2) + block, low),
            dma((tp_size - 1, 2)),
            dma((tp_size - 1, 2)),
            dma((tp_size - 1, 2)),
            dma((tp_size - 1, 2)),
        ],
        compiler_params=pltpu.CompilerParams(
            collective_id=0, has_side_effects=True, vmem_limit_bytes=63 * 1024 * 1024
        ),
    )(queries, key_rows, value_matrix, attention_out, output_grad, w_query, key_weight, value_weight, span_pos)


def solution(mesh):
    in_specs = (
        P("ctx", "tp"),
        P("ctx", "tp"),
        P("ctx", "tp"),
        P("ctx", "tp"),
        P("ctx", "tp"),
        P(None, "tp"),
        P(None, "tp"),
        P(None, "tp"),
        P(),
    )
    body = functools.partial(local, mesh.shape["ctx"], mesh.shape["tp"])
    return jax.shard_map(body, mesh=mesh, in_specs=in_specs, out_specs=P("ctx", "tp"), check_vma=False)
```

```python
import functools

import jax
import jax.numpy as jnp
from jax import lax
from jax.experimental import pallas as pl
from jax.experimental.pallas import tpu as pltpu
from jax.sharding import PartitionSpec as P

HEAD_SIZE = 128
PAIR = 2
SCORE_SCALE = HEAD_SIZE ** (-0.5)
LOG2_E = 1.4426950408889634
MESH = pl.DeviceIdType.MESH


def nt_dot(left, right):
    return lax.dot_general(
        left, right, (((1,), (1,)), ((), ())), preferred_element_type=jnp.float32
    )


def nn_dot(left, right):
    return lax.dot_general(
        left, right, (((1,), (0,)), ((), ())), preferred_element_type=jnp.float32
    )


def tn_dot(left, right):
    return lax.dot_general(
        left, right, (((0,), (0,)), ((), ())), preferred_element_type=jnp.float32
    )


def each(count, body):
    if count <= 8:
        for index in range(count):
            body(index)
    else:
        lax.fori_loop(0, count, lambda index, _: (body(index), 0)[1], 0)


def kernel(
    ctx_size,
    tp_size,
    q_ref,
    k_ref,
    v_ref,
    o_ref,
    g_ref,
    wq_ref,
    wk_ref,
    wv_ref,
    pos_ref,
    out_ref,
    q_in,
    g_in,
    o_in,
    wq,
    w_kv,
    kv,
    q_rows,
    g_rows,
    delta,
    scores,
    grad_scores,
    row_max,
    row_sum,
    dq_t,
    pair_out,
    pair_in,
    own_part,
    far_out,
    far_in,
    tp_out,
    tp_in,
    local_sem,
    kv_send,
    kv_fwd,
    kv_recv,
    pair_send,
    pair_recv,
    far_send,
    far_recv,
    tp_send,
    tp_recv,
    g_kv,
    w_send,
    w_recv,
    g_send,
    g_recv,
):
    rows = q_ref.shape[0]
    span = rows // 2
    heads = q_ref.shape[1] // HEAD_SIZE
    query_rows = heads * rows
    far_size = ctx_size // PAIR
    features = out_ref.shape[1]
    chunk = min(far_size, 4)
    chunks = far_size // chunk
    chunk_rows = chunk * rows

    c = lax.axis_index("ctx")
    t = lax.axis_index("tp")
    a = lax.div(c, PAIR)
    b = lax.rem(c, PAIR)
    partner = (a * PAIR + 1 - b, t)

    def far(step):
        return lax.rem(a + step, far_size)

    def far_device(other):
        return (other * PAIR + b, t)

    def feature_rows(owner):
        return pl.ds(pl.multiple_of(owner * features, features), features)

    def tp_peer(step):
        return lax.rem(t + step, tp_size)

    own_features = feature_rows(t)
    order = sorted(range(1, tp_size), key=lambda step: abs(step - tp_size // 2))

    local_pairs = [
        (q_ref, q_in),
        (g_ref, g_in),
        (o_ref, o_in),
        (k_ref, kv.at[0, b, a]),
        (v_ref, kv.at[1, b, a]),
        (wq_ref, wq),
        (wk_ref.at[own_features], w_kv.at[t, 0]),
        (wv_ref.at[own_features], w_kv.at[t, 1]),
    ]
    local_copies = [
        pltpu.make_async_copy(src, dst, local_sem.at[i]) for i, (src, dst) in enumerate(local_pairs)
    ]
    for copy in local_copies:
        copy.start()

    barrier = pltpu.get_barrier_semaphore()

    def greet_far(i):
        pl.semaphore_signal(barrier, inc=1, device_id=far_device(far(i + 1)), device_id_type=MESH)

    each(far_size - 1, greet_far)
    pl.semaphore_signal(barrier, inc=1, device_id=partner, device_id_type=MESH)
    for step in range(1, tp_size):
        pl.semaphore_signal(
            barrier, inc=1, device_id=(c, lax.rem(t + step, tp_size)), device_id_type=MESH
        )
    pl.semaphore_wait(barrier, far_size - 1 + 1 + tp_size - 1)

    def direct_copy(kind, i):
        return pltpu.make_async_remote_copy(
            src_ref=(k_ref, v_ref)[kind],
            dst_ref=kv.at[kind, b, a],
            send_sem=kv_send.at[kind, i],
            recv_sem=kv_recv.at[kind, b, a],
            device_id=far_device(far(i + 1)),
            device_id_type=MESH,
        )

    def own_forward(kind):
        return pltpu.make_async_remote_copy(
            src_ref=(k_ref, v_ref)[kind],
            dst_ref=kv.at[kind, b, a],
            send_sem=kv_fwd.at[kind, a],
            recv_sem=kv_recv.at[kind, b, a],
            device_id=partner,
            device_id_type=MESH,
        )

    def forward(kind, group, other):
        return pltpu.make_async_remote_copy(
            src_ref=kv.at[kind, group, other],
            dst_ref=kv.at[kind, group, other],
            send_sem=kv_fwd.at[kind, other],
            recv_sem=kv_recv.at[kind, group, other],
            device_id=partner,
            device_id_type=MESH,
        )

    for kind in range(2):
        each(far_size - 1, lambda i, kind=kind: direct_copy(kind, i).start())
        own_forward(kind).start()

    def weight_copy(step, kind):
        return pltpu.make_async_remote_copy(
            src_ref=(wk_ref, wv_ref)[kind].at[feature_rows(tp_peer(step))],
            dst_ref=w_kv.at[t, kind],
            send_sem=w_send.at[step - 1, kind],
            recv_sem=w_recv.at[step - 1, kind],
            device_id=(c, tp_peer(step)),
            device_id_type=MESH,
        )

    for kind in (1, 0):
        for step in order:
            weight_copy(step, kind).start()

    for copy in local_copies[:3]:
        copy.wait()
    for head in range(heads):
        lanes = slice(head * HEAD_SIZE, (head + 1) * HEAD_SIZE)
        held = slice(head * rows, (head + 1) * rows)
        q_rows[held, :] = q_in[:, lanes]
        g_head = g_in[:, lanes]
        g_rows[held, :] = g_head
        products = g_head.astype(jnp.float32) * o_in[:, lanes].astype(jnp.float32)
        delta[:, held] = jnp.sum(products.T, axis=0, keepdims=True)

    lane = lax.rem(lax.broadcasted_iota(jnp.int32, (1, query_rows), 1), rows)
    query_pos = lane + jnp.where(
        lane < span, pos_ref[PAIR * c] * span, pos_ref[PAIR * c + 1] * span - span
    )
    key_offset = lax.broadcasted_iota(jnp.int32, (span, 1), 0)

    row_max[...] = jnp.full_like(row_max, -jnp.inf)
    row_sum[...] = jnp.zeros_like(row_sum)
    dq_t[...] = jnp.zeros_like(dq_t)

    def score_block(which, group, other):
        raw = nt_dot(kv[0, group, other], q_rows[...]) * (SCORE_SCALE * LOG2_E)
        best = row_max[which]
        for part in range(2):
            key_pos = pos_ref[2 * (other * PAIR + group) + part] * span + key_offset
            masked = jnp.where(key_pos <= query_pos, raw[part * span : (part + 1) * span], -jnp.inf)
            scores[which, other, part * span : (part + 1) * span, :] = masked
            best = jnp.maximum(best, jnp.max(masked, axis=0, keepdims=True))
        row_max[which] = best

    def exp_block(which, other):
        weights = jnp.exp2(scores[which, other] - row_max[which])
        scores[which, other] = weights
        row_sum[which] += jnp.sum(weights, axis=0, keepdims=True)

    def value_block(which, other, factor):
        probs = scores[which, other] * factor
        scores[which, other] = probs
        part = nn_dot(probs.astype(jnp.bfloat16), g_rows[...])
        target = pair_out if which == 1 else own_part
        target[1, other] = part.astype(target.dtype)

    def key_block(which, group, other):
        grad_probs = nt_dot(kv[1, group, other], g_rows[...])
        grads = (scores[which, other] * (grad_probs - delta[...])).astype(jnp.bfloat16)
        grad_scores[which, other] = grads
        part = nn_dot(grads, q_rows[...]) * SCORE_SCALE
        target = pair_out if which == 1 else own_part
        target[0, other] = part.astype(target.dtype)

    def query_chunk(which, group, index):
        at = pl.ds(index * chunk, chunk)
        keys = kv[0, group, at].reshape(chunk_rows, HEAD_SIZE)
        dq_t[...] += tn_dot(keys, grad_scores[which, at].reshape(chunk_rows, query_rows))

    def key_arrival(i):
        other = far(i + 1)
        forward(0, b, other).wait_recv()
        forward(0, b, other).start()
        score_block(0, b, other)

    def value_arrival(i):
        other = far(i + 1)
        forward(1, b, other).wait_recv()
        forward(1, b, other).start()

    def pair_key_arrival(i):
        other = far(i)
        forward(0, 1 - b, other).wait_recv()
        score_block(1, 1 - b, other)

    local_copies[3].wait()
    score_block(0, b, a)
    each(far_size - 1, key_arrival)
    each(far_size - 1, value_arrival)
    each(far_size, lambda i: exp_block(0, i))
    each(far_size, pair_key_arrival)
    row_max[1] = jnp.maximum(row_max[0], row_max[1])
    each(far_size, lambda i: exp_block(1, i))
    own_shrink = jnp.exp2(row_max[0] - row_max[1])
    pair_factor = 1.0 / (row_sum[0] * own_shrink + row_sum[1])
    own_factor = own_shrink * pair_factor
    local_copies[4].wait()

    def pair_copy(kind, other):
        return pltpu.make_async_remote_copy(
            src_ref=pair_out.at[kind, other],
            dst_ref=pair_in.at[kind, other],
            send_sem=pair_send.at[kind, other],
            recv_sem=pair_recv.at[kind, other],
            device_id=partner,
            device_id_type=MESH,
        )

    def far_copy(kind, i):
        return pltpu.make_async_remote_copy(
            src_ref=far_out.at[kind, i],
            dst_ref=far_in.at[kind, i],
            send_sem=far_send.at[kind, i],
            recv_sem=far_recv.at[kind, i],
            device_id=far_device(far(i + 1)),
            device_id_type=MESH,
        )

    def send_far(kind, i):
        other = far(i + 1)
        pair_copy(kind, other).wait_recv()
        far_out[kind, i] = (
            own_part[kind, other] + pair_in[kind, other].astype(jnp.float32)
        ).astype(jnp.bfloat16)
        far_copy(kind, i).start()

    def pair_value(i):
        other = far(i + 1)
        value_block(1, other, pair_factor)
        pair_copy(1, other).start()

    def pair_key(i):
        other = far(i + 1)
        forward(1, 1 - b, other).wait_recv()
        key_block(1, 1 - b, other)
        pair_copy(0, other).start()

    each(far_size, pair_value)
    each(far_size, lambda i: value_block(0, i, own_factor))
    each(far_size, pair_key)
    each(far_size, lambda i: key_block(0, b, i))
    each(far_size - 1, lambda i: send_far(1, i))

    each(chunks, lambda i: query_chunk(1, 1 - b, i))
    each(chunks, lambda i: query_chunk(0, b, i))
    local_copies[5].wait()
    grad_query = (dq_t[...] * SCORE_SCALE).astype(jnp.bfloat16)
    stacked = jnp.concatenate(
        [grad_query[:, head * rows : (head + 1) * rows] for head in range(heads)], axis=0
    )

    def tp_copy(step):
        return pltpu.make_async_remote_copy(
            src_ref=tp_out.at[step - 1],
            dst_ref=tp_in.at[step - 1],
            send_sem=tp_send.at[step - 1],
            recv_sem=tp_recv.at[step - 1],
            device_id=(c, tp_peer(step)),
            device_id_type=MESH,
        )

    for step in order:
        tp_out[step - 1] = nn_dot(wq[feature_rows(tp_peer(step)), :], stacked).astype(jnp.bfloat16)
        tp_copy(step).start()
    each(far_size - 1, lambda i: send_far(0, i))
    own_proj = nn_dot(wq[own_features, :], stacked)

    def grad_copy(step, kind):
        return pltpu.make_async_remote_copy(
            src_ref=g_kv.at[t, kind],
            dst_ref=g_kv.at[t, kind],
            send_sem=g_send.at[step - 1, kind],
            recv_sem=g_recv.at[step - 1, kind],
            device_id=(c, tp_peer(step)),
            device_id_type=MESH,
        )

    def add_far(kind, i):
        far_copy(kind, i).wait_recv()
        own_part[kind, a] += far_in[kind, i].astype(jnp.float32)

    def finish(kind):
        pair_copy(kind, a).wait_recv()
        own_part[kind, a] += pair_in[kind, a].astype(jnp.float32)
        each(far_size - 1, lambda i: add_far(kind, i))
        g_kv[t, kind] = own_part[kind, a].astype(jnp.bfloat16)
        for step in order:
            grad_copy(step, kind).start()

    finish(1)
    for step in reversed(order):
        tp_copy(step).wait_recv()
        own_proj += tp_in[step - 1].astype(jnp.float32)
    total = own_proj.T
    finish(0)
    for kind in (1, 0):
        local_copies[6 + kind].wait()
        total += nt_dot(g_kv[t, kind], w_kv[t, kind])
        for step in reversed(order):
            sender = lax.rem(t + tp_size - step, tp_size)
            weight_copy(step, kind).wait_recv()
            grad_copy(step, kind).wait_recv()
            total += nt_dot(g_kv[sender, kind], w_kv[sender, kind])
    out_ref[...] = total.astype(out_ref.dtype)

    for kind in range(2):
        each(far_size - 1, lambda i, kind=kind: direct_copy(kind, i).wait_send())
        each(far_size, lambda i, kind=kind: forward(kind, b, i).wait_send())
        each(far_size, lambda i, kind=kind: pair_copy(kind, i).wait_send())
        each(far_size - 1, lambda i, kind=kind: far_copy(kind, i).wait_send())
        for step in order:
            weight_copy(step, kind).wait_send()
            grad_copy(step, kind).wait_send()
    for step in order:
        tp_copy(step).wait_send()


def local(ctx_size, tp_size, queries, key_rows, value_matrix, attention_out, output_grad, w_query, key_weight, value_weight, span_pos):
    rows, width = queries.shape
    model = w_query.shape[0]
    query_rows = rows * (width // HEAD_SIZE)
    far_size = ctx_size // PAIR
    features = model // tp_size
    block = (rows, HEAD_SIZE)
    low, full = jnp.bfloat16, jnp.float32
    dma = pltpu.SemaphoreType.DMA
    in_hbm = pl.BlockSpec(memory_space=pltpu.HBM)
    return pl.pallas_call(
        functools.partial(kernel, ctx_size, tp_size),
        out_shape=pltpu.VMEM((rows, features), low),
        in_specs=[in_hbm] * 8 + [pl.BlockSpec(memory_space=pltpu.SMEM)],
        out_specs=pl.BlockSpec(memory_space=pltpu.VMEM),
        scratch_shapes=[
            pltpu.VMEM((rows, width), low),
            pltpu.VMEM((rows, width), low),
            pltpu.VMEM((rows, width), low),
            pltpu.VMEM(w_query.shape, low),
            pltpu.VMEM((tp_size, 2, features, HEAD_SIZE), low),
            pltpu.VMEM((2, PAIR, far_size) + block, low),
            pltpu.VMEM((query_rows, HEAD_SIZE), low),
            pltpu.VMEM((query_rows, HEAD_SIZE), low),
            pltpu.VMEM((1, query_rows), full),
            pltpu.VMEM((PAIR, far_size, rows, query_rows), full),
            pltpu.VMEM((PAIR, far_size, rows, query_rows), low),
            pltpu.VMEM((PAIR, 1, query_rows), full),
            pltpu.VMEM((PAIR, 1, query_rows), full),
            pltpu.VMEM((HEAD_SIZE, query_rows), full),
            pltpu.VMEM((2, far_size) + block, low),
            pltpu.VMEM((2, far_size) + block, low),
            pltpu.VMEM((2, far_size) + block, full),
            pltpu.VMEM((2, far_size - 1) + block, low),
            pltpu.VMEM((2, far_size - 1) + block, low),
            pltpu.VMEM((tp_size - 1, features, rows), low),
            pltpu.VMEM((tp_size - 1, features, rows), low),
            dma((8,)),
            dma((2, far_size - 1)),
            dma((2, far_size)),
            dma((2, PAIR, far_size)),
            dma((2, far_size)),
            dma((2, far_size)),
            dma((2, far_size - 1)),
            dma((2, far_size - 1)),
            dma((tp_size - 1,)),
            dma((tp_size - 1,)),
            pltpu.VMEM((tp_size, 2) + block, low),
            dma((tp_size - 1, 2)),
            dma((tp_size - 1, 2)),
            dma((tp_size - 1, 2)),
            dma((tp_size - 1, 2)),
        ],
        compiler_params=pltpu.CompilerParams(
            collective_id=0, has_side_effects=True, vmem_limit_bytes=(65536 - 192) * 1024
        ),
    )(queries, key_rows, value_matrix, attention_out, output_grad, w_query, key_weight, value_weight, span_pos)


def solution(mesh):
    in_specs = (
        P("ctx", "tp"),
        P("ctx", "tp"),
        P("ctx", "tp"),
        P("ctx", "tp"),
        P("ctx", "tp"),
        P(None, "tp"),
        P(None, "tp"),
        P(None, "tp"),
        P(),
    )
    body = functools.partial(local, mesh.shape["ctx"], mesh.shape["tp"])
    return jax.shard_map(body, mesh=mesh, in_specs=in_specs, out_specs=P("ctx", "tp"), check_vma=False)
```

```python
import functools

import jax
import jax.numpy as jnp
from jax import lax
from jax.experimental import pallas as pl
from jax.experimental.pallas import tpu as pltpu
from jax.sharding import PartitionSpec as P

HEAD_SIZE = 128
PAIR = 2
SCORE_SCALE = HEAD_SIZE ** (-0.5)
LOG2_E = 1.4426950408889634
MESH = pl.DeviceIdType.MESH


def nt_dot(left, right):
    return lax.dot_general(
        left, right, (((1,), (1,)), ((), ())), preferred_element_type=jnp.float32
    )


def nn_dot(left, right):
    return lax.dot_general(
        left, right, (((1,), (0,)), ((), ())), preferred_element_type=jnp.float32
    )


def tn_dot(left, right):
    return lax.dot_general(
        left, right, (((0,), (0,)), ((), ())), preferred_element_type=jnp.float32
    )


def each(count, body):
    if count <= 8:
        for index in range(count):
            body(index)
    else:
        lax.fori_loop(0, count, lambda index, _: (body(index), 0)[1], 0)


def kernel(
    ctx_size,
    tp_size,
    q_ref,
    k_ref,
    v_ref,
    o_ref,
    g_ref,
    wq_ref,
    wk_ref,
    wv_ref,
    pos_ref,
    out_ref,
    q_in,
    g_in,
    o_in,
    wq,
    w_kv,
    kv,
    q_rows,
    g_rows,
    delta,
    scores,
    grad_scores,
    row_max,
    row_sum,
    dq_t,
    pair_out,
    pair_in,
    own_part,
    far_out,
    far_in,
    tp_pair_out,
    tp_pair_in,
    tp_out,
    tp_in,
    local_sem,
    kv_send,
    kv_fwd,
    kv_recv,
    pair_send,
    pair_recv,
    far_send,
    far_recv,
    tp_pair_send,
    tp_pair_recv,
    tp_send,
    tp_recv,
    g_kv,
    w_send,
    w_recv,
    g_send,
    g_recv,
):
    rows = q_ref.shape[0]
    span = rows // 2
    heads = q_ref.shape[1] // HEAD_SIZE
    query_rows = heads * rows
    far_size = ctx_size // PAIR
    features = out_ref.shape[1]
    chunk = min(far_size, 4)
    chunks = far_size // chunk
    chunk_rows = chunk * rows

    c = lax.axis_index("ctx")
    t = lax.axis_index("tp")
    a = lax.div(c, PAIR)
    b = lax.rem(c, PAIR)
    partner = (a * PAIR + 1 - b, t)

    def far(step):
        return lax.rem(a + step, far_size)

    def far_device(other):
        return (other * PAIR + b, t)

    def feature_rows(owner):
        return pl.ds(pl.multiple_of(owner * features, features), features)

    def tp_peer(step):
        return lax.rem(t + step, tp_size)

    tp_rows = tp_size // PAIR
    t_row = lax.div(t, PAIR)
    t_core = lax.rem(t, PAIR)

    def tp_row(step):
        return lax.rem(t_row + step, tp_rows)

    own_features = feature_rows(t)
    order = sorted(range(1, tp_size), key=lambda step: abs(step - tp_size // 2))

    local_pairs = [
        (q_ref, q_in),
        (g_ref, g_in),
        (o_ref, o_in),
        (k_ref, kv.at[0, b, a]),
        (v_ref, kv.at[1, b, a]),
        (wq_ref, wq),
        (wk_ref.at[own_features], w_kv.at[t, 0]),
        (wv_ref.at[own_features], w_kv.at[t, 1]),
    ]
    local_copies = [
        pltpu.make_async_copy(src, dst, local_sem.at[i]) for i, (src, dst) in enumerate(local_pairs)
    ]
    for copy in local_copies:
        copy.start()

    barrier = pltpu.get_barrier_semaphore()

    def greet_far(i):
        pl.semaphore_signal(barrier, inc=1, device_id=far_device(far(i + 1)), device_id_type=MESH)

    each(far_size - 1, greet_far)
    pl.semaphore_signal(barrier, inc=1, device_id=partner, device_id_type=MESH)
    for step in range(1, tp_size):
        pl.semaphore_signal(
            barrier, inc=1, device_id=(c, lax.rem(t + step, tp_size)), device_id_type=MESH
        )
    pl.semaphore_wait(barrier, far_size - 1 + 1 + tp_size - 1)

    def direct_copy(kind, i):
        return pltpu.make_async_remote_copy(
            src_ref=(k_ref, v_ref)[kind],
            dst_ref=kv.at[kind, b, a],
            send_sem=kv_send.at[kind, i],
            recv_sem=kv_recv.at[kind, b, a],
            device_id=far_device(far(i + 1)),
            device_id_type=MESH,
        )

    def own_forward(kind):
        return pltpu.make_async_remote_copy(
            src_ref=(k_ref, v_ref)[kind],
            dst_ref=kv.at[kind, b, a],
            send_sem=kv_fwd.at[kind, a],
            recv_sem=kv_recv.at[kind, b, a],
            device_id=partner,
            device_id_type=MESH,
        )

    def forward(kind, group, other):
        return pltpu.make_async_remote_copy(
            src_ref=kv.at[kind, group, other],
            dst_ref=kv.at[kind, group, other],
            send_sem=kv_fwd.at[kind, other],
            recv_sem=kv_recv.at[kind, group, other],
            device_id=partner,
            device_id_type=MESH,
        )

    for kind in range(2):
        each(far_size - 1, lambda i, kind=kind: direct_copy(kind, i).start())
        own_forward(kind).start()

    def weight_copy(step, kind):
        return pltpu.make_async_remote_copy(
            src_ref=(wk_ref, wv_ref)[kind].at[feature_rows(tp_peer(step))],
            dst_ref=w_kv.at[t, kind],
            send_sem=w_send.at[step - 1, kind],
            recv_sem=w_recv.at[step - 1, kind],
            device_id=(c, tp_peer(step)),
            device_id_type=MESH,
        )

    for kind in (1, 0):
        for step in order:
            weight_copy(step, kind).start()

    for copy in local_copies[:3]:
        copy.wait()
    for head in range(heads):
        lanes = slice(head * HEAD_SIZE, (head + 1) * HEAD_SIZE)
        held = slice(head * rows, (head + 1) * rows)
        q_rows[held, :] = q_in[:, lanes]
        g_head = g_in[:, lanes]
        g_rows[held, :] = g_head
        products = g_head.astype(jnp.float32) * o_in[:, lanes].astype(jnp.float32)
        delta[:, held] = jnp.sum(products.T, axis=0, keepdims=True)

    lane = lax.rem(lax.broadcasted_iota(jnp.int32, (1, query_rows), 1), rows)
    query_pos = lane + jnp.where(
        lane < span, pos_ref[PAIR * c] * span, pos_ref[PAIR * c + 1] * span - span
    )
    key_offset = lax.broadcasted_iota(jnp.int32, (span, 1), 0)

    row_max[...] = jnp.full_like(row_max, -jnp.inf)
    row_sum[...] = jnp.zeros_like(row_sum)
    dq_t[...] = jnp.zeros_like(dq_t)

    def score_block(which, group, other):
        raw = nt_dot(kv[0, group, other], q_rows[...]) * (SCORE_SCALE * LOG2_E)
        best = row_max[which]
        for part in range(2):
            key_pos = pos_ref[2 * (other * PAIR + group) + part] * span + key_offset
            masked = jnp.where(key_pos <= query_pos, raw[part * span : (part + 1) * span], -jnp.inf)
            scores[which, other, part * span : (part + 1) * span, :] = masked
            best = jnp.maximum(best, jnp.max(masked, axis=0, keepdims=True))
        row_max[which] = best

    def exp_block(which, other):
        weights = jnp.exp2(scores[which, other] - row_max[which])
        scores[which, other] = weights
        row_sum[which] += jnp.sum(weights, axis=0, keepdims=True)

    def value_block(which, other, factor):
        probs = scores[which, other] * factor
        scores[which, other] = probs
        part = nn_dot(probs.astype(jnp.bfloat16), g_rows[...])
        target = pair_out if which == 1 else own_part
        target[1, other] = part.astype(target.dtype)

    def key_block(which, group, other):
        grad_probs = nt_dot(kv[1, group, other], g_rows[...])
        grads = (scores[which, other] * (grad_probs - delta[...])).astype(jnp.bfloat16)
        grad_scores[which, other] = grads
        part = nn_dot(grads, q_rows[...]) * SCORE_SCALE
        target = pair_out if which == 1 else own_part
        target[0, other] = part.astype(target.dtype)

    def query_chunk(which, group, index):
        at = pl.ds(index * chunk, chunk)
        keys = kv[0, group, at].reshape(chunk_rows, HEAD_SIZE)
        dq_t[...] += tn_dot(keys, grad_scores[which, at].reshape(chunk_rows, query_rows))

    def key_arrival(i):
        other = far(i + 1)
        forward(0, b, other).wait_recv()
        forward(0, b, other).start()
        score_block(0, b, other)

    def value_arrival(i):
        other = far(i + 1)
        forward(1, b, other).wait_recv()
        forward(1, b, other).start()

    def pair_key_arrival(i):
        other = far(i)
        forward(0, 1 - b, other).wait_recv()
        score_block(1, 1 - b, other)

    local_copies[3].wait()
    score_block(0, b, a)
    each(far_size - 1, key_arrival)
    each(far_size - 1, value_arrival)
    each(far_size, lambda i: exp_block(0, i))
    each(far_size, pair_key_arrival)
    row_max[1] = jnp.maximum(row_max[0], row_max[1])
    each(far_size, lambda i: exp_block(1, i))
    own_shrink = jnp.exp2(row_max[0] - row_max[1])
    pair_factor = 1.0 / (row_sum[0] * own_shrink + row_sum[1])
    own_factor = own_shrink * pair_factor
    local_copies[4].wait()

    def pair_copy(kind, other):
        return pltpu.make_async_remote_copy(
            src_ref=pair_out.at[kind, other],
            dst_ref=pair_in.at[kind, other],
            send_sem=pair_send.at[kind, other],
            recv_sem=pair_recv.at[kind, other],
            device_id=partner,
            device_id_type=MESH,
        )

    def far_copy(kind, i):
        return pltpu.make_async_remote_copy(
            src_ref=far_out.at[kind, i],
            dst_ref=far_in.at[kind, i],
            send_sem=far_send.at[kind, i],
            recv_sem=far_recv.at[kind, i],
            device_id=far_device(far(i + 1)),
            device_id_type=MESH,
        )

    def send_far(kind, i):
        other = far(i + 1)
        pair_copy(kind, other).wait_recv()
        far_out[kind, i] = (
            own_part[kind, other] + pair_in[kind, other].astype(jnp.float32)
        ).astype(jnp.bfloat16)
        far_copy(kind, i).start()

    def pair_value(i):
        other = far(i + 1)
        value_block(1, other, pair_factor)
        pair_copy(1, other).start()

    def pair_key(i):
        other = far(i + 1)
        forward(1, 1 - b, other).wait_recv()
        key_block(1, 1 - b, other)
        pair_copy(0, other).start()

    each(far_size, pair_value)
    each(far_size, lambda i: value_block(0, i, own_factor))
    each(far_size, pair_key)
    each(far_size, lambda i: key_block(0, b, i))
    each(far_size - 1, lambda i: send_far(1, i))

    each(chunks, lambda i: query_chunk(1, 1 - b, i))
    each(chunks, lambda i: query_chunk(0, b, i))
    local_copies[5].wait()
    grad_query = (dq_t[...] * SCORE_SCALE).astype(jnp.bfloat16)
    stacked = jnp.concatenate(
        [grad_query[:, head * rows : (head + 1) * rows] for head in range(heads)], axis=0
    )

    def tp_pair_copy(row):
        return pltpu.make_async_remote_copy(
            src_ref=tp_pair_out.at[row],
            dst_ref=tp_pair_in.at[row],
            send_sem=tp_pair_send.at[row],
            recv_sem=tp_pair_recv.at[row],
            device_id=(c, t_row * PAIR + 1 - t_core),
            device_id_type=MESH,
        )

    def tp_copy(step):
        return pltpu.make_async_remote_copy(
            src_ref=tp_out.at[step - 1],
            dst_ref=tp_in.at[step - 1],
            send_sem=tp_send.at[step - 1],
            recv_sem=tp_recv.at[step - 1],
            device_id=(c, tp_row(step) * PAIR + t_core),
            device_id_type=MESH,
        )

    def query_part(owner):
        return nn_dot(wq[feature_rows(owner), :], stacked)

    for step in range(1, tp_rows + 1):
        row = tp_row(step)
        tp_pair_out[row] = query_part(row * PAIR + 1 - t_core).astype(jnp.bfloat16)
        tp_pair_copy(row).start()
    for step in range(1, tp_rows):
        row = tp_row(step)
        part = query_part(row * PAIR + t_core)
        tp_pair_copy(row).wait_recv()
        tp_out[step - 1] = (part + tp_pair_in[row].astype(jnp.float32)).astype(jnp.bfloat16)
        tp_copy(step).start()
    each(far_size - 1, lambda i: send_far(0, i))
    own_proj = query_part(t)

    def grad_copy(step, kind):
        return pltpu.make_async_remote_copy(
            src_ref=g_kv.at[t, kind],
            dst_ref=g_kv.at[t, kind],
            send_sem=g_send.at[step - 1, kind],
            recv_sem=g_recv.at[step - 1, kind],
            device_id=(c, tp_peer(step)),
            device_id_type=MESH,
        )

    def add_far(kind, i):
        far_copy(kind, i).wait_recv()
        own_part[kind, a] += far_in[kind, i].astype(jnp.float32)

    def finish(kind):
        pair_copy(kind, a).wait_recv()
        own_part[kind, a] += pair_in[kind, a].astype(jnp.float32)
        each(far_size - 1, lambda i: add_far(kind, i))
        g_kv[t, kind] = own_part[kind, a].astype(jnp.bfloat16)
        for step in order:
            grad_copy(step, kind).start()

    finish(1)
    tp_pair_copy(t_row).wait_recv()
    own_proj += tp_pair_in[t_row].astype(jnp.float32)
    for step in range(1, tp_rows):
        tp_copy(step).wait_recv()
        own_proj += tp_in[step - 1].astype(jnp.float32)
    total = own_proj.T
    finish(0)
    for kind in (1, 0):
        local_copies[6 + kind].wait()
        total += nt_dot(g_kv[t, kind], w_kv[t, kind])
        for step in reversed(order):
            sender = lax.rem(t + tp_size - step, tp_size)
            weight_copy(step, kind).wait_recv()
            grad_copy(step, kind).wait_recv()
            total += nt_dot(g_kv[sender, kind], w_kv[sender, kind])
    out_ref[...] = total.astype(out_ref.dtype)

    for kind in range(2):
        each(far_size - 1, lambda i, kind=kind: direct_copy(kind, i).wait_send())
        each(far_size, lambda i, kind=kind: forward(kind, b, i).wait_send())
        each(far_size, lambda i, kind=kind: pair_copy(kind, i).wait_send())
        each(far_size - 1, lambda i, kind=kind: far_copy(kind, i).wait_send())
        for step in order:
            weight_copy(step, kind).wait_send()
            grad_copy(step, kind).wait_send()
    for row in range(tp_rows):
        tp_pair_copy(row).wait_send()
    for step in range(1, tp_rows):
        tp_copy(step).wait_send()


def local(ctx_size, tp_size, queries, key_rows, value_matrix, attention_out, output_grad, w_query, key_weight, value_weight, span_pos):
    rows, width = queries.shape
    model = w_query.shape[0]
    query_rows = rows * (width // HEAD_SIZE)
    far_size = ctx_size // PAIR
    features = model // tp_size
    block = (rows, HEAD_SIZE)
    low, full = jnp.bfloat16, jnp.float32
    dma = pltpu.SemaphoreType.DMA
    in_hbm = pl.BlockSpec(memory_space=pltpu.HBM)
    return pl.pallas_call(
        functools.partial(kernel, ctx_size, tp_size),
        out_shape=pltpu.VMEM((rows, features), low),
        in_specs=[in_hbm] * 8 + [pl.BlockSpec(memory_space=pltpu.SMEM)],
        out_specs=pl.BlockSpec(memory_space=pltpu.VMEM),
        scratch_shapes=[
            pltpu.VMEM((rows, width), low),
            pltpu.VMEM((rows, width), low),
            pltpu.VMEM((rows, width), low),
            pltpu.VMEM(w_query.shape, low),
            pltpu.VMEM((tp_size, 2, features, HEAD_SIZE), low),
            pltpu.VMEM((2, PAIR, far_size) + block, low),
            pltpu.VMEM((query_rows, HEAD_SIZE), low),
            pltpu.VMEM((query_rows, HEAD_SIZE), low),
            pltpu.VMEM((1, query_rows), full),
            pltpu.VMEM((PAIR, far_size, rows, query_rows), full),
            pltpu.VMEM((PAIR, far_size, rows, query_rows), low),
            pltpu.VMEM((PAIR, 1, query_rows), full),
            pltpu.VMEM((PAIR, 1, query_rows), full),
            pltpu.VMEM((HEAD_SIZE, query_rows), full),
            pltpu.VMEM((2, far_size) + block, low),
            pltpu.VMEM((2, far_size) + block, low),
            pltpu.VMEM((2, far_size) + block, full),
            pltpu.VMEM((2, far_size - 1) + block, low),
            pltpu.VMEM((2, far_size - 1) + block, low),
            pltpu.VMEM((tp_size // PAIR, features, rows), low),
            pltpu.VMEM((tp_size // PAIR, features, rows), low),
            pltpu.VMEM((tp_size // PAIR - 1, features, rows), low),
            pltpu.VMEM((tp_size // PAIR - 1, features, rows), low),
            dma((8,)),
            dma((2, far_size - 1)),
            dma((2, far_size)),
            dma((2, PAIR, far_size)),
            dma((2, far_size)),
            dma((2, far_size)),
            dma((2, far_size - 1)),
            dma((2, far_size - 1)),
            dma((tp_size // PAIR,)),
            dma((tp_size // PAIR,)),
            dma((tp_size // PAIR - 1,)),
            dma((tp_size // PAIR - 1,)),
            pltpu.VMEM((tp_size, 2) + block, low),
            dma((tp_size - 1, 2)),
            dma((tp_size - 1, 2)),
            dma((tp_size - 1, 2)),
            dma((tp_size - 1, 2)),
        ],
        compiler_params=pltpu.CompilerParams(
            collective_id=0, has_side_effects=True, vmem_limit_bytes=(65536 - 192) * 1024
        ),
    )(queries, key_rows, value_matrix, attention_out, output_grad, w_query, key_weight, value_weight, span_pos)


def solution(mesh):
    in_specs = (
        P("ctx", "tp"),
        P("ctx", "tp"),
        P("ctx", "tp"),
        P("ctx", "tp"),
        P("ctx", "tp"),
        P(None, "tp"),
        P(None, "tp"),
        P(None, "tp"),
        P(),
    )
    body = functools.partial(local, mesh.shape["ctx"], mesh.shape["tp"])
    return jax.shard_map(body, mesh=mesh, in_specs=in_specs, out_specs=P("ctx", "tp"), check_vma=False)
```

```python
import functools

import jax
import jax.numpy as jnp
from jax import lax
from jax.experimental import pallas as pl
from jax.experimental.pallas import tpu as pltpu
from jax.sharding import PartitionSpec as P

HEAD_SIZE = 128
PAIR = 2
SCORE_SCALE = HEAD_SIZE ** (-0.5)
LOG2_E = 1.4426950408889634
MESH = pl.DeviceIdType.MESH


def nn_dot(left, right):
    return lax.dot_general(
        left, right, (((1,), (0,)), ((), ())), preferred_element_type=jnp.float32
    )


def tn_dot(left, right):
    return lax.dot_general(
        left, right, (((0,), (0,)), ((), ())), preferred_element_type=jnp.float32
    )


def each(count, body):
    if count <= 8:
        for index in range(count):
            body(index)
    else:
        lax.fori_loop(0, count, lambda index, _: (body(index), 0)[1], 0)


def kernel(
    ctx_size,
    tp_size,
    q_ref,
    k_ref,
    v_ref,
    o_ref,
    g_ref,
    wq_ref,
    wk_ref,
    wv_ref,
    pos_ref,
    out_ref,
    q_in,
    g_in,
    o_in,
    wq,
    w_kv,
    kv,
    q_rows,
    g_rows,
    q_cols,
    g_cols,
    delta,
    scores,
    grad_scores,
    row_max,
    row_sum,
    dq_t,
    pair_out,
    pair_in,
    own_part,
    far_out,
    far_in,
    tp_out,
    tp_in,
    local_sem,
    kv_send,
    kv_fwd,
    kv_recv,
    pair_send,
    pair_recv,
    far_send,
    far_recv,
    tp_send,
    tp_recv,
    g_kv,
    w_send,
    w_recv,
    g_send,
    g_recv,
):
    rows = q_ref.shape[0]
    span = rows // 2
    heads = q_ref.shape[1] // HEAD_SIZE
    query_rows = heads * rows
    far_size = ctx_size // PAIR
    features = out_ref.shape[1]
    chunk = min(far_size, 4)
    chunks = far_size // chunk
    chunk_rows = chunk * rows

    c = lax.axis_index("ctx")
    t = lax.axis_index("tp")
    a = lax.div(c, PAIR)
    b = lax.rem(c, PAIR)
    partner = (a * PAIR + 1 - b, t)

    def far(step):
        return lax.rem(a + step, far_size)

    def far_device(other):
        return (other * PAIR + b, t)

    def feature_rows(owner):
        return pl.ds(pl.multiple_of(owner * features, features), features)

    def tp_peer(step):
        return lax.rem(t + step, tp_size)

    own_features = feature_rows(t)
    order = sorted(range(1, tp_size), key=lambda step: abs(step - tp_size // 2))

    local_pairs = [
        (q_ref, q_in),
        (g_ref, g_in),
        (o_ref, o_in),
        (k_ref, kv.at[0, b, a]),
        (v_ref, kv.at[1, b, a]),
        (wq_ref, wq),
        (wk_ref.at[own_features], w_kv.at[t, 0]),
        (wv_ref.at[own_features], w_kv.at[t, 1]),
    ]
    local_copies = [
        pltpu.make_async_copy(src, dst, local_sem.at[i]) for i, (src, dst) in enumerate(local_pairs)
    ]
    for copy in local_copies:
        copy.start()

    barrier = pltpu.get_barrier_semaphore()

    def greet_far(i):
        pl.semaphore_signal(barrier, inc=1, device_id=far_device(far(i + 1)), device_id_type=MESH)

    each(far_size - 1, greet_far)
    pl.semaphore_signal(barrier, inc=1, device_id=partner, device_id_type=MESH)
    for step in range(1, tp_size):
        pl.semaphore_signal(
            barrier, inc=1, device_id=(c, lax.rem(t + step, tp_size)), device_id_type=MESH
        )
    pl.semaphore_wait(barrier, far_size - 1 + 1 + tp_size - 1)

    def direct_copy(kind, i):
        return pltpu.make_async_remote_copy(
            src_ref=(k_ref, v_ref)[kind],
            dst_ref=kv.at[kind, b, a],
            send_sem=kv_send.at[kind, i],
            recv_sem=kv_recv.at[kind, b, a],
            device_id=far_device(far(i + 1)),
            device_id_type=MESH,
        )

    def own_forward(kind):
        return pltpu.make_async_remote_copy(
            src_ref=(k_ref, v_ref)[kind],
            dst_ref=kv.at[kind, b, a],
            send_sem=kv_fwd.at[kind, a],
            recv_sem=kv_recv.at[kind, b, a],
            device_id=partner,
            device_id_type=MESH,
        )

    def forward(kind, group, other):
        return pltpu.make_async_remote_copy(
            src_ref=kv.at[kind, group, other],
            dst_ref=kv.at[kind, group, other],
            send_sem=kv_fwd.at[kind, other],
            recv_sem=kv_recv.at[kind, group, other],
            device_id=partner,
            device_id_type=MESH,
        )

    for kind in range(2):
        each(far_size - 1, lambda i, kind=kind: direct_copy(kind, i).start())
        own_forward(kind).start()

    def weight_copy(step, kind):
        return pltpu.make_async_remote_copy(
            src_ref=(wk_ref, wv_ref)[kind].at[feature_rows(tp_peer(step))],
            dst_ref=w_kv.at[t, kind],
            send_sem=w_send.at[step - 1, kind],
            recv_sem=w_recv.at[step - 1, kind],
            device_id=(c, tp_peer(step)),
            device_id_type=MESH,
        )

    for kind in (1, 0):
        for step in order:
            weight_copy(step, kind).start()

    for copy in local_copies[:3]:
        copy.wait()
    for head in range(heads):
        lanes = slice(head * HEAD_SIZE, (head + 1) * HEAD_SIZE)
        held = slice(head * rows, (head + 1) * rows)
        q_rows[held, :] = q_in[:, lanes]
        q_cols[:, held] = q_in[:, lanes].T
        g_head = g_in[:, lanes]
        g_rows[held, :] = g_head
        g_cols[:, held] = g_head.T
        products = g_head.astype(jnp.float32) * o_in[:, lanes].astype(jnp.float32)
        delta[:, held] = jnp.sum(products.T, axis=0, keepdims=True)

    lane = lax.rem(lax.broadcasted_iota(jnp.int32, (1, query_rows), 1), rows)
    query_pos = lane + jnp.where(
        lane < span, pos_ref[PAIR * c] * span, pos_ref[PAIR * c + 1] * span - span
    )
    key_offset = lax.broadcasted_iota(jnp.int32, (span, 1), 0)

    row_max[...] = jnp.full_like(row_max, -jnp.inf)
    row_sum[...] = jnp.zeros_like(row_sum)
    dq_t[...] = jnp.zeros_like(dq_t)

    def score_block(which, group, other):
        raw = nn_dot(kv[0, group, other], q_cols[...]) * (SCORE_SCALE * LOG2_E)
        best = row_max[which]
        for part in range(2):
            key_pos = pos_ref[2 * (other * PAIR + group) + part] * span + key_offset
            masked = jnp.where(key_pos <= query_pos, raw[part * span : (part + 1) * span], -jnp.inf)
            scores[which, other, part * span : (part + 1) * span, :] = masked
            best = jnp.maximum(best, jnp.max(masked, axis=0, keepdims=True))
        row_max[which] = best

    def exp_block(which, other):
        weights = jnp.exp2(scores[which, other] - row_max[which])
        scores[which, other] = weights
        row_sum[which] += jnp.sum(weights, axis=0, keepdims=True)

    def value_block(which, other, factor):
        probs = scores[which, other] * factor
        scores[which, other] = probs
        part = nn_dot(probs.astype(jnp.bfloat16), g_rows[...])
        target = pair_out if which == 1 else own_part
        target[1, other] = part.astype(target.dtype)

    def key_block(which, group, other):
        grad_probs = nn_dot(kv[1, group, other], g_cols[...])
        grads = (scores[which, other] * (grad_probs - delta[...])).astype(jnp.bfloat16)
        grad_scores[which, other] = grads
        part = nn_dot(grads, q_rows[...]) * SCORE_SCALE
        target = pair_out if which == 1 else own_part
        target[0, other] = part.astype(target.dtype)

    def query_chunk(which, group, index):
        at = pl.ds(index * chunk, chunk)
        keys = kv[0, group, at].reshape(chunk_rows, HEAD_SIZE)
        dq_t[...] += tn_dot(keys, grad_scores[which, at].reshape(chunk_rows, query_rows))

    def key_arrival(i):
        other = far(i + 1)
        forward(0, b, other).wait_recv()
        forward(0, b, other).start()
        score_block(0, b, other)

    def value_arrival(i):
        other = far(i + 1)
        forward(1, b, other).wait_recv()
        forward(1, b, other).start()

    def pair_key_arrival(i):
        other = far(i)
        forward(0, 1 - b, other).wait_recv()
        score_block(1, 1 - b, other)

    local_copies[3].wait()
    score_block(0, b, a)
    each(far_size - 1, key_arrival)
    each(far_size - 1, value_arrival)
    each(far_size, lambda i: exp_block(0, i))
    each(far_size, pair_key_arrival)
    row_max[1] = jnp.maximum(row_max[0], row_max[1])
    each(far_size, lambda i: exp_block(1, i))
    own_shrink = jnp.exp2(row_max[0] - row_max[1])
    pair_factor = 1.0 / (row_sum[0] * own_shrink + row_sum[1])
    own_factor = own_shrink * pair_factor
    local_copies[4].wait()

    def pair_copy(kind, other):
        return pltpu.make_async_remote_copy(
            src_ref=pair_out.at[kind, other],
            dst_ref=pair_in.at[kind, other],
            send_sem=pair_send.at[kind, other],
            recv_sem=pair_recv.at[kind, other],
            device_id=partner,
            device_id_type=MESH,
        )

    def far_copy(kind, i):
        return pltpu.make_async_remote_copy(
            src_ref=far_out.at[kind, i],
            dst_ref=far_in.at[kind, i],
            send_sem=far_send.at[kind, i],
            recv_sem=far_recv.at[kind, i],
            device_id=far_device(far(i + 1)),
            device_id_type=MESH,
        )

    def send_far(kind, i):
        other = far(i + 1)
        pair_copy(kind, other).wait_recv()
        far_out[kind, i] = (
            own_part[kind, other] + pair_in[kind, other].astype(jnp.float32)
        ).astype(jnp.bfloat16)
        far_copy(kind, i).start()

    def pair_value(i):
        other = far(i + 1)
        value_block(1, other, pair_factor)
        pair_copy(1, other).start()

    def pair_key(i):
        other = far(i + 1)
        forward(1, 1 - b, other).wait_recv()
        key_block(1, 1 - b, other)
        pair_copy(0, other).start()

    each(far_size, pair_value)
    each(far_size, lambda i: value_block(0, i, own_factor))
    each(far_size, pair_key)
    each(far_size, lambda i: key_block(0, b, i))
    each(far_size - 1, lambda i: send_far(1, i))

    each(chunks, lambda i: query_chunk(1, 1 - b, i))
    each(chunks, lambda i: query_chunk(0, b, i))
    local_copies[5].wait()
    grad_query = (dq_t[...] * SCORE_SCALE).astype(jnp.bfloat16)
    stacked = jnp.concatenate(
        [grad_query[:, head * rows : (head + 1) * rows] for head in range(heads)], axis=0
    )

    def tp_copy(step):
        return pltpu.make_async_remote_copy(
            src_ref=tp_out.at[step - 1],
            dst_ref=tp_in.at[step - 1],
            send_sem=tp_send.at[step - 1],
            recv_sem=tp_recv.at[step - 1],
            device_id=(c, tp_peer(step)),
            device_id_type=MESH,
        )

    for step in order:
        tp_out[step - 1] = nn_dot(wq[feature_rows(tp_peer(step)), :], stacked).astype(jnp.bfloat16)
        tp_copy(step).start()
    each(far_size - 1, lambda i: send_far(0, i))
    own_proj = nn_dot(wq[own_features, :], stacked)

    def grad_copy(step, kind):
        return pltpu.make_async_remote_copy(
            src_ref=g_kv.at[t, kind],
            dst_ref=g_kv.at[t, kind],
            send_sem=g_send.at[step - 1, kind],
            recv_sem=g_recv.at[step - 1, kind],
            device_id=(c, tp_peer(step)),
            device_id_type=MESH,
        )

    def add_far(kind, i):
        far_copy(kind, i).wait_recv()
        own_part[kind, a] += far_in[kind, i].astype(jnp.float32)

    def finish(kind):
        pair_copy(kind, a).wait_recv()
        own_part[kind, a] += pair_in[kind, a].astype(jnp.float32)
        each(far_size - 1, lambda i: add_far(kind, i))
        g_kv[t, kind] = own_part[kind, a].T.astype(jnp.bfloat16)
        for step in order:
            grad_copy(step, kind).start()

    finish(1)
    for step in reversed(order):
        tp_copy(step).wait_recv()
        own_proj += tp_in[step - 1].astype(jnp.float32)
    for kind in range(2):
        each(far_size - 1, lambda i, kind=kind: direct_copy(kind, i).wait_send())
        each(far_size, lambda i, kind=kind: forward(kind, b, i).wait_send())
        each(far_size, lambda i, kind=kind: pair_copy(kind, i).wait_send())
        local_copies[6 + kind].wait()
        for step in order:
            weight_copy(step, kind).wait_recv()
            weight_copy(step, kind).wait_send()
    for step in order:
        tp_copy(step).wait_send()
    finish(0)
    total = own_proj
    for kind in (1, 0):
        total += nn_dot(w_kv[t, kind], g_kv[t, kind])
        for step in reversed(order):
            sender = lax.rem(t + tp_size - step, tp_size)
            grad_copy(step, kind).wait_recv()
            total += nn_dot(w_kv[sender, kind], g_kv[sender, kind])
    out_ref[...] = total.T.astype(out_ref.dtype)

    for kind in range(2):
        each(far_size - 1, lambda i, kind=kind: far_copy(kind, i).wait_send())
        for step in order:
            grad_copy(step, kind).wait_send()


def local(ctx_size, tp_size, queries, key_rows, value_matrix, attention_out, output_grad, w_query, key_weight, value_weight, span_pos):
    rows, width = queries.shape
    model = w_query.shape[0]
    query_rows = rows * (width // HEAD_SIZE)
    far_size = ctx_size // PAIR
    features = model // tp_size
    block = (rows, HEAD_SIZE)
    low, full = jnp.bfloat16, jnp.float32
    dma = pltpu.SemaphoreType.DMA
    in_hbm = pl.BlockSpec(memory_space=pltpu.HBM)
    return pl.pallas_call(
        functools.partial(kernel, ctx_size, tp_size),
        out_shape=pltpu.VMEM((rows, features), low),
        in_specs=[in_hbm] * 8 + [pl.BlockSpec(memory_space=pltpu.SMEM)],
        out_specs=pl.BlockSpec(memory_space=pltpu.VMEM),
        scratch_shapes=[
            pltpu.VMEM((rows, width), low),
            pltpu.VMEM((rows, width), low),
            pltpu.VMEM((rows, width), low),
            pltpu.VMEM(w_query.shape, low),
            pltpu.VMEM((tp_size, 2, features, HEAD_SIZE), low),
            pltpu.VMEM((2, PAIR, far_size) + block, low),
            pltpu.VMEM((query_rows, HEAD_SIZE), low),
            pltpu.VMEM((query_rows, HEAD_SIZE), low),
            pltpu.VMEM((HEAD_SIZE, query_rows), low),
            pltpu.VMEM((HEAD_SIZE, query_rows), low),
            pltpu.VMEM((1, query_rows), full),
            pltpu.VMEM((PAIR, far_size, rows, query_rows), full),
            pltpu.VMEM((PAIR, far_size, rows, query_rows), low),
            pltpu.VMEM((PAIR, 1, query_rows), full),
            pltpu.VMEM((PAIR, 1, query_rows), full),
            pltpu.VMEM((HEAD_SIZE, query_rows), full),
            pltpu.VMEM((2, far_size) + block, low),
            pltpu.VMEM((2, far_size) + block, low),
            pltpu.VMEM((2, far_size) + block, full),
            pltpu.VMEM((2, far_size - 1) + block, low),
            pltpu.VMEM((2, far_size - 1) + block, low),
            pltpu.VMEM((tp_size - 1, features, rows), low),
            pltpu.VMEM((tp_size - 1, features, rows), low),
            dma((8,)),
            dma((2, far_size - 1)),
            dma((2, far_size)),
            dma((2, PAIR, far_size)),
            dma((2, far_size)),
            dma((2, far_size)),
            dma((2, far_size - 1)),
            dma((2, far_size - 1)),
            dma((tp_size - 1,)),
            dma((tp_size - 1,)),
            pltpu.VMEM((tp_size, 2, HEAD_SIZE, rows), low),
            dma((tp_size - 1, 2)),
            dma((tp_size - 1, 2)),
            dma((tp_size - 1, 2)),
            dma((tp_size - 1, 2)),
        ],
        compiler_params=pltpu.CompilerParams(
            collective_id=0, has_side_effects=True, vmem_limit_bytes=(65536 - 192) * 1024
        ),
    )(queries, key_rows, value_matrix, attention_out, output_grad, w_query, key_weight, value_weight, span_pos)


def solution(mesh):
    in_specs = (
        P("ctx", "tp"),
        P("ctx", "tp"),
        P("ctx", "tp"),
        P("ctx", "tp"),
        P("ctx", "tp"),
        P(None, "tp"),
        P(None, "tp"),
        P(None, "tp"),
        P(),
    )
    body = functools.partial(local, mesh.shape["ctx"], mesh.shape["tp"])
    return jax.shard_map(body, mesh=mesh, in_specs=in_specs, out_specs=P("ctx", "tp"), check_vma=False)
```

```python
import functools

import jax
import jax.numpy as jnp
from jax import lax
from jax.experimental import pallas as pl
from jax.experimental.pallas import tpu as pltpu
from jax.sharding import PartitionSpec as P

HEAD_SIZE = 128
PAIR = 2
SCORE_SCALE = HEAD_SIZE ** (-0.5)
LOG2_E = 1.4426950408889634
MESH = pl.DeviceIdType.MESH


def nn_dot(left, right):
    return lax.dot_general(
        left, right, (((1,), (0,)), ((), ())), preferred_element_type=jnp.float32
    )


def tn_dot(left, right):
    return lax.dot_general(
        left, right, (((0,), (0,)), ((), ())), preferred_element_type=jnp.float32
    )


def each(count, body):
    if count <= 8:
        for index in range(count):
            body(index)
    else:
        lax.fori_loop(0, count, lambda index, _: (body(index), 0)[1], 0)


def kernel(
    ctx_size,
    tp_size,
    q_ref,
    k_ref,
    v_ref,
    o_ref,
    g_ref,
    wq_ref,
    wk_ref,
    wv_ref,
    pos_ref,
    out_ref,
    q_in,
    g_in,
    o_in,
    wq,
    w_kv,
    kv,
    q_rows,
    g_rows,
    q_cols,
    g_cols,
    delta,
    scores,
    grad_scores,
    row_max,
    row_sum,
    dq_t,
    pair_out,
    pair_in,
    own_part,
    far_out,
    far_in,
    tp_out,
    tp_in,
    local_sem,
    kv_send,
    kv_fwd,
    kv_recv,
    pair_send,
    pair_recv,
    far_send,
    far_recv,
    tp_send,
    tp_recv,
    g_kv,
    w_send,
    w_recv,
    g_send,
    g_recv,
):
    rows = q_ref.shape[0]
    span = rows // 2
    heads = q_ref.shape[1] // HEAD_SIZE
    query_rows = heads * rows
    far_size = ctx_size // PAIR
    features = out_ref.shape[1]
    chunk = min(far_size, 4)
    chunks = far_size // chunk
    chunk_rows = chunk * rows

    c = lax.axis_index("ctx")
    t = lax.axis_index("tp")
    a = lax.div(c, PAIR)
    b = lax.rem(c, PAIR)
    partner = (a * PAIR + 1 - b, t)

    def far(step):
        return lax.rem(a + step, far_size)

    def far_device(other):
        return (other * PAIR + b, t)

    def feature_rows(owner):
        return pl.ds(pl.multiple_of(owner * features, features), features)

    def tp_peer(step):
        return lax.rem(t + step, tp_size)

    own_features = feature_rows(t)
    order = sorted(range(1, tp_size), key=lambda step: abs(step - tp_size // 2))

    local_pairs = [
        (q_ref, q_in),
        (g_ref, g_in),
        (o_ref, o_in),
        (k_ref, kv.at[0, b, a]),
        (v_ref, kv.at[1, b, a]),
        (wq_ref, wq),
        (wk_ref.at[own_features], w_kv.at[t, 0]),
        (wv_ref.at[own_features], w_kv.at[t, 1]),
    ]
    local_copies = [
        pltpu.make_async_copy(src, dst, local_sem.at[i]) for i, (src, dst) in enumerate(local_pairs)
    ]
    for copy in local_copies:
        copy.start()

    barrier = pltpu.get_barrier_semaphore()

    def greet_far(i):
        pl.semaphore_signal(barrier, inc=1, device_id=far_device(far(i + 1)), device_id_type=MESH)

    each(far_size - 1, greet_far)
    pl.semaphore_signal(barrier, inc=1, device_id=partner, device_id_type=MESH)
    for step in range(1, tp_size):
        pl.semaphore_signal(
            barrier, inc=1, device_id=(c, lax.rem(t + step, tp_size)), device_id_type=MESH
        )
    pl.semaphore_wait(barrier, far_size - 1 + 1 + tp_size - 1)

    def direct_copy(kind, i):
        return pltpu.make_async_remote_copy(
            src_ref=(k_ref, v_ref)[kind],
            dst_ref=kv.at[kind, b, a],
            send_sem=kv_send.at[kind, i],
            recv_sem=kv_recv.at[kind, b, a],
            device_id=far_device(far(i + 1)),
            device_id_type=MESH,
        )

    def own_forward(kind):
        return pltpu.make_async_remote_copy(
            src_ref=(k_ref, v_ref)[kind],
            dst_ref=kv.at[kind, b, a],
            send_sem=kv_fwd.at[kind, a],
            recv_sem=kv_recv.at[kind, b, a],
            device_id=partner,
            device_id_type=MESH,
        )

    def forward(kind, group, other):
        return pltpu.make_async_remote_copy(
            src_ref=kv.at[kind, group, other],
            dst_ref=kv.at[kind, group, other],
            send_sem=kv_fwd.at[kind, other],
            recv_sem=kv_recv.at[kind, group, other],
            device_id=partner,
            device_id_type=MESH,
        )

    def send_own(kind):
        own_forward(kind).start()
        each(far_size - 1, lambda i: direct_copy(kind, i).start())

    send_own(0)

    def weight_copy(step, kind):
        return pltpu.make_async_remote_copy(
            src_ref=(wk_ref, wv_ref)[kind].at[feature_rows(tp_peer(step))],
            dst_ref=w_kv.at[t, kind],
            send_sem=w_send.at[step - 1, kind],
            recv_sem=w_recv.at[step - 1, kind],
            device_id=(c, tp_peer(step)),
            device_id_type=MESH,
        )

    def send_weights(kind):
        for step in order:
            weight_copy(step, kind).start()

    for copy in local_copies[:3]:
        copy.wait()
    for head in range(heads):
        lanes = slice(head * HEAD_SIZE, (head + 1) * HEAD_SIZE)
        held = slice(head * rows, (head + 1) * rows)
        q_rows[held, :] = q_in[:, lanes]
        q_cols[:, held] = q_in[:, lanes].T
        g_head = g_in[:, lanes]
        g_rows[held, :] = g_head
        g_cols[:, held] = g_head.T
        products = g_head.astype(jnp.float32) * o_in[:, lanes].astype(jnp.float32)
        delta[:, held] = jnp.sum(products.T, axis=0, keepdims=True)

    lane = lax.rem(lax.broadcasted_iota(jnp.int32, (1, query_rows), 1), rows)
    query_pos = lane + jnp.where(
        lane < span, pos_ref[PAIR * c] * span, pos_ref[PAIR * c + 1] * span - span
    )
    key_offset = lax.broadcasted_iota(jnp.int32, (span, 1), 0)

    row_max[...] = jnp.full_like(row_max, -jnp.inf)
    row_sum[...] = jnp.zeros_like(row_sum)
    dq_t[...] = jnp.zeros_like(dq_t)

    def score_block(which, group, other):
        raw = nn_dot(kv[0, group, other], q_cols[...]) * (SCORE_SCALE * LOG2_E)
        best = row_max[which]
        for part in range(2):
            key_pos = pos_ref[2 * (other * PAIR + group) + part] * span + key_offset
            masked = jnp.where(key_pos <= query_pos, raw[part * span : (part + 1) * span], -jnp.inf)
            scores[which, other, part * span : (part + 1) * span, :] = masked
            best = jnp.maximum(best, jnp.max(masked, axis=0, keepdims=True))
        row_max[which] = best

    def exp_block(which, other):
        weights = jnp.exp2(scores[which, other] - row_max[which])
        scores[which, other] = weights
        row_sum[which] += jnp.sum(weights, axis=0, keepdims=True)

    def value_block(which, other, factor):
        probs = scores[which, other] * factor
        scores[which, other] = probs
        part = nn_dot(probs.astype(jnp.bfloat16), g_rows[...])
        target = pair_out if which == 1 else own_part
        target[1, other] = part.astype(target.dtype)

    def key_block(which, group, other):
        grad_probs = nn_dot(kv[1, group, other], g_cols[...])
        grads = (scores[which, other] * (grad_probs - delta[...])).astype(jnp.bfloat16)
        grad_scores[which, other] = grads
        part = nn_dot(grads, q_rows[...]) * SCORE_SCALE
        target = pair_out if which == 1 else own_part
        target[0, other] = part.astype(target.dtype)

    def query_chunk(which, group, index):
        at = pl.ds(index * chunk, chunk)
        keys = kv[0, group, at].reshape(chunk_rows, HEAD_SIZE)
        dq_t[...] += tn_dot(keys, grad_scores[which, at].reshape(chunk_rows, query_rows))

    def key_arrival(i):
        other = far(i + 1)
        forward(0, b, other).wait_recv()
        forward(0, b, other).start()
        score_block(0, b, other)

    def value_arrival(i):
        other = far(i + 1)
        forward(1, b, other).wait_recv()
        forward(1, b, other).start()

    def pair_key_arrival(i):
        other = far(i)
        forward(0, 1 - b, other).wait_recv()
        score_block(1, 1 - b, other)

    local_copies[3].wait()
    score_block(0, b, a)
    each(far_size - 1, key_arrival)
    send_own(1)
    send_weights(1)
    each(far_size, lambda i: exp_block(0, i))
    each(far_size, pair_key_arrival)
    each(far_size - 1, value_arrival)
    send_weights(0)
    row_max[1] = jnp.maximum(row_max[0], row_max[1])
    each(far_size, lambda i: exp_block(1, i))
    own_shrink = jnp.exp2(row_max[0] - row_max[1])
    pair_factor = 1.0 / (row_sum[0] * own_shrink + row_sum[1])
    own_factor = own_shrink * pair_factor
    local_copies[4].wait()

    def pair_copy(kind, other):
        return pltpu.make_async_remote_copy(
            src_ref=pair_out.at[kind, other],
            dst_ref=pair_in.at[kind, other],
            send_sem=pair_send.at[kind, other],
            recv_sem=pair_recv.at[kind, other],
            device_id=partner,
            device_id_type=MESH,
        )

    def far_copy(kind, i):
        return pltpu.make_async_remote_copy(
            src_ref=far_out.at[kind, i],
            dst_ref=far_in.at[kind, i],
            send_sem=far_send.at[kind, i],
            recv_sem=far_recv.at[kind, i],
            device_id=far_device(far(i + 1)),
            device_id_type=MESH,
        )

    def send_far(kind, i):
        other = far(i + 1)
        pair_copy(kind, other).wait_recv()
        far_out[kind, i] = (
            own_part[kind, other] + pair_in[kind, other].astype(jnp.float32)
        ).astype(jnp.bfloat16)
        far_copy(kind, i).start()

    def pair_value(i):
        other = far(i + 1)
        value_block(1, other, pair_factor)
        pair_copy(1, other).start()

    def pair_key(i):
        other = far(i + 1)
        forward(1, 1 - b, other).wait_recv()
        key_block(1, 1 - b, other)
        pair_copy(0, other).start()

    each(far_size, pair_value)
    each(far_size, lambda i: value_block(0, i, own_factor))
    each(far_size, pair_key)
    each(far_size, lambda i: key_block(0, b, i))
    each(far_size - 1, lambda i: send_far(1, i))

    each(chunks, lambda i: query_chunk(1, 1 - b, i))
    each(chunks, lambda i: query_chunk(0, b, i))
    local_copies[5].wait()
    grad_query = (dq_t[...] * SCORE_SCALE).astype(jnp.bfloat16)
    stacked = jnp.concatenate(
        [grad_query[:, head * rows : (head + 1) * rows] for head in range(heads)], axis=0
    )

    def tp_copy(step):
        return pltpu.make_async_remote_copy(
            src_ref=tp_out.at[step - 1],
            dst_ref=tp_in.at[step - 1],
            send_sem=tp_send.at[step - 1],
            recv_sem=tp_recv.at[step - 1],
            device_id=(c, tp_peer(step)),
            device_id_type=MESH,
        )

    for step in order:
        tp_out[step - 1] = nn_dot(wq[feature_rows(tp_peer(step)), :], stacked).astype(jnp.bfloat16)
        tp_copy(step).start()
    each(far_size - 1, lambda i: send_far(0, i))
    own_proj = nn_dot(wq[own_features, :], stacked)

    def grad_copy(step, kind):
        return pltpu.make_async_remote_copy(
            src_ref=g_kv.at[t, kind],
            dst_ref=g_kv.at[t, kind],
            send_sem=g_send.at[step - 1, kind],
            recv_sem=g_recv.at[step - 1, kind],
            device_id=(c, tp_peer(step)),
            device_id_type=MESH,
        )

    def add_far(kind, i):
        far_copy(kind, i).wait_recv()
        own_part[kind, a] += far_in[kind, i].astype(jnp.float32)

    def finish(kind):
        pair_copy(kind, a).wait_recv()
        own_part[kind, a] += pair_in[kind, a].astype(jnp.float32)
        each(far_size - 1, lambda i: add_far(kind, i))
        g_kv[t, kind] = own_part[kind, a].T.astype(jnp.bfloat16)
        for step in order:
            grad_copy(step, kind).start()

    finish(1)
    for step in reversed(order):
        tp_copy(step).wait_recv()
        own_proj += tp_in[step - 1].astype(jnp.float32)
    for kind in range(2):
        each(far_size - 1, lambda i, kind=kind: direct_copy(kind, i).wait_send())
        each(far_size, lambda i, kind=kind: forward(kind, b, i).wait_send())
        each(far_size, lambda i, kind=kind: pair_copy(kind, i).wait_send())
        local_copies[6 + kind].wait()
        for step in order:
            weight_copy(step, kind).wait_recv()
            weight_copy(step, kind).wait_send()
    for step in order:
        tp_copy(step).wait_send()
    finish(0)
    total = own_proj
    for kind in (1, 0):
        total += nn_dot(w_kv[t, kind], g_kv[t, kind])
        for step in reversed(order):
            sender = lax.rem(t + tp_size - step, tp_size)
            grad_copy(step, kind).wait_recv()
            total += nn_dot(w_kv[sender, kind], g_kv[sender, kind])
    out_ref[...] = total.T.astype(out_ref.dtype)

    for kind in range(2):
        each(far_size - 1, lambda i, kind=kind: far_copy(kind, i).wait_send())
        for step in order:
            grad_copy(step, kind).wait_send()


def local(ctx_size, tp_size, queries, key_rows, value_matrix, attention_out, output_grad, w_query, key_weight, value_weight, span_pos):
    rows, width = queries.shape
    model = w_query.shape[0]
    query_rows = rows * (width // HEAD_SIZE)
    far_size = ctx_size // PAIR
    features = model // tp_size
    block = (rows, HEAD_SIZE)
    low, full = jnp.bfloat16, jnp.float32
    dma = pltpu.SemaphoreType.DMA
    in_hbm = pl.BlockSpec(memory_space=pltpu.HBM)
    return pl.pallas_call(
        functools.partial(kernel, ctx_size, tp_size),
        out_shape=pltpu.VMEM((rows, features), low),
        in_specs=[in_hbm] * 8 + [pl.BlockSpec(memory_space=pltpu.SMEM)],
        out_specs=pl.BlockSpec(memory_space=pltpu.VMEM),
        scratch_shapes=[
            pltpu.VMEM((rows, width), low),
            pltpu.VMEM((rows, width), low),
            pltpu.VMEM((rows, width), low),
            pltpu.VMEM(w_query.shape, low),
            pltpu.VMEM((tp_size, 2, features, HEAD_SIZE), low),
            pltpu.VMEM((2, PAIR, far_size) + block, low),
            pltpu.VMEM((query_rows, HEAD_SIZE), low),
            pltpu.VMEM((query_rows, HEAD_SIZE), low),
            pltpu.VMEM((HEAD_SIZE, query_rows), low),
            pltpu.VMEM((HEAD_SIZE, query_rows), low),
            pltpu.VMEM((1, query_rows), full),
            pltpu.VMEM((PAIR, far_size, rows, query_rows), full),
            pltpu.VMEM((PAIR, far_size, rows, query_rows), low),
            pltpu.VMEM((PAIR, 1, query_rows), full),
            pltpu.VMEM((PAIR, 1, query_rows), full),
            pltpu.VMEM((HEAD_SIZE, query_rows), full),
            pltpu.VMEM((2, far_size) + block, low),
            pltpu.VMEM((2, far_size) + block, low),
            pltpu.VMEM((2, far_size) + block, full),
            pltpu.VMEM((2, far_size - 1) + block, low),
            pltpu.VMEM((2, far_size - 1) + block, low),
            pltpu.VMEM((tp_size - 1, features, rows), low),
            pltpu.VMEM((tp_size - 1, features, rows), low),
            dma((8,)),
            dma((2, far_size - 1)),
            dma((2, far_size)),
            dma((2, PAIR, far_size)),
            dma((2, far_size)),
            dma((2, far_size)),
            dma((2, far_size - 1)),
            dma((2, far_size - 1)),
            dma((tp_size - 1,)),
            dma((tp_size - 1,)),
            pltpu.VMEM((tp_size, 2, HEAD_SIZE, rows), low),
            dma((tp_size - 1, 2)),
            dma((tp_size - 1, 2)),
            dma((tp_size - 1, 2)),
            dma((tp_size - 1, 2)),
        ],
        compiler_params=pltpu.CompilerParams(
            collective_id=0, has_side_effects=True, vmem_limit_bytes=(65536 - 192) * 1024
        ),
    )(queries, key_rows, value_matrix, attention_out, output_grad, w_query, key_weight, value_weight, span_pos)


def solution(mesh):
    in_specs = (
        P("ctx", "tp"),
        P("ctx", "tp"),
        P("ctx", "tp"),
        P("ctx", "tp"),
        P("ctx", "tp"),
        P(None, "tp"),
        P(None, "tp"),
        P(None, "tp"),
        P(),
    )
    body = functools.partial(local, mesh.shape["ctx"], mesh.shape["tp"])
    return jax.shard_map(body, mesh=mesh, in_specs=in_specs, out_specs=P("ctx", "tp"), check_vma=False)
```

```python
import functools

import jax
import jax.numpy as jnp
from jax import lax
from jax.experimental import pallas as pl
from jax.experimental.pallas import tpu as pltpu
from jax.sharding import PartitionSpec as P

HEAD_SIZE = 128
PAIR = 2
SCORE_SCALE = HEAD_SIZE ** (-0.5)
LOG2_E = 1.4426950408889634
MESH = pl.DeviceIdType.MESH


def nn_dot(left, right):
    return lax.dot_general(
        left, right, (((1,), (0,)), ((), ())), preferred_element_type=jnp.float32
    )


def tn_dot(left, right):
    return lax.dot_general(
        left, right, (((0,), (0,)), ((), ())), preferred_element_type=jnp.float32
    )


def each(count, body):
    if count <= 8:
        for index in range(count):
            body(index)
    else:
        lax.fori_loop(0, count, lambda index, _: (body(index), 0)[1], 0)


def kernel(
    ctx_size,
    tp_size,
    q_ref,
    k_ref,
    v_ref,
    o_ref,
    g_ref,
    wq_ref,
    wk_ref,
    wv_ref,
    pos_ref,
    out_ref,
    q_in,
    g_in,
    o_in,
    wq,
    w_kv,
    kv,
    q_rows,
    g_rows,
    q_cols,
    g_cols,
    delta,
    scores,
    grad_scores,
    row_max,
    row_sum,
    dq_t,
    pair_out,
    pair_in,
    own_part,
    far_out,
    far_in,
    tp_out,
    tp_in,
    local_sem,
    kv_send,
    kv_fwd,
    kv_recv,
    pair_send,
    pair_recv,
    far_send,
    far_recv,
    tp_send,
    tp_recv,
    g_kv,
    w_send,
    w_recv,
    g_send,
    g_recv,
    across_send,
):
    rows = q_ref.shape[0]
    span = rows // 2
    heads = q_ref.shape[1] // HEAD_SIZE
    query_rows = heads * rows
    far_size = ctx_size // PAIR
    features = out_ref.shape[1]
    chunk = min(far_size, 4)
    chunks = far_size // chunk
    chunk_rows = chunk * rows

    c = lax.axis_index("ctx")
    t = lax.axis_index("tp")
    a = lax.div(c, PAIR)
    b = lax.rem(c, PAIR)
    partner = (a * PAIR + 1 - b, t)

    def far(step):
        other, bit = a, 1
        while bit < far_size:
            other = other + (step // bit % 2) * bit * (1 - 2 * (a // bit % 2))
            bit *= 2
        return other

    def far_device(other):
        return (other * PAIR + b, t)

    def feature_rows(owner):
        return pl.ds(pl.multiple_of(owner * features, features), features)

    def tp_peer(step):
        return lax.rem(t + step, tp_size)

    own_features = feature_rows(t)
    order = sorted(range(1, tp_size), key=lambda step: abs(step - tp_size // 2))

    local_pairs = [
        (q_ref, q_in),
        (g_ref, g_in),
        (o_ref, o_in),
        (k_ref, kv.at[0, b, a]),
        (v_ref, kv.at[1, b, a]),
        (wq_ref, wq),
        (wk_ref.at[own_features], w_kv.at[t, 0]),
        (wv_ref.at[own_features], w_kv.at[t, 1]),
    ]
    local_copies = [
        pltpu.make_async_copy(src, dst, local_sem.at[i]) for i, (src, dst) in enumerate(local_pairs)
    ]
    for copy in local_copies:
        copy.start()

    barrier = pltpu.get_barrier_semaphore()

    def greet_far(i):
        pl.semaphore_signal(barrier, inc=1, device_id=far_device(far(i + 1)), device_id_type=MESH)

    each(far_size - 1, greet_far)
    pl.semaphore_signal(barrier, inc=1, device_id=partner, device_id_type=MESH)
    for step in range(1, tp_size):
        pl.semaphore_signal(
            barrier, inc=1, device_id=(c, lax.rem(t + step, tp_size)), device_id_type=MESH
        )
    pl.semaphore_wait(barrier, far_size - 1 + 1 + tp_size - 1)

    def direct_copy(kind, i):
        return pltpu.make_async_remote_copy(
            src_ref=(k_ref, v_ref)[kind],
            dst_ref=kv.at[kind, b, a],
            send_sem=kv_send.at[kind, i],
            recv_sem=kv_recv.at[kind, b, a],
            device_id=far_device(far(i + 1)),
            device_id_type=MESH,
        )

    def own_forward(kind):
        return pltpu.make_async_remote_copy(
            src_ref=(k_ref, v_ref)[kind],
            dst_ref=kv.at[kind, b, a],
            send_sem=kv_fwd.at[kind, a],
            recv_sem=kv_recv.at[kind, b, a],
            device_id=partner,
            device_id_type=MESH,
        )

    def forward(kind, group, other):
        return pltpu.make_async_remote_copy(
            src_ref=kv.at[kind, group, other],
            dst_ref=kv.at[kind, group, other],
            send_sem=kv_fwd.at[kind, other],
            recv_sem=kv_recv.at[kind, group, other],
            device_id=partner,
            device_id_type=MESH,
        )

    for kind in range(2):
        each(far_size - 1, lambda i, kind=kind: direct_copy(kind, i).start())
        own_forward(kind).start()

    def weight_copy(step, kind):
        return pltpu.make_async_remote_copy(
            src_ref=(wk_ref, wv_ref)[kind].at[feature_rows(tp_peer(step))],
            dst_ref=w_kv.at[t, kind],
            send_sem=w_send.at[step - 1, kind],
            recv_sem=w_recv.at[step - 1, kind],
            device_id=(c, tp_peer(step)),
            device_id_type=MESH,
        )

    for kind in (1, 0):
        for step in order:
            weight_copy(step, kind).start()

    for copy in local_copies[:3]:
        copy.wait()
    for head in range(heads):
        lanes = slice(head * HEAD_SIZE, (head + 1) * HEAD_SIZE)
        held = slice(head * rows, (head + 1) * rows)
        q_rows[held, :] = q_in[:, lanes]
        q_cols[:, held] = q_in[:, lanes].T
        g_head = g_in[:, lanes]
        g_rows[held, :] = g_head
        g_cols[:, held] = g_head.T
        products = g_head.astype(jnp.float32) * o_in[:, lanes].astype(jnp.float32)
        delta[:, held] = jnp.sum(products.T, axis=0, keepdims=True)

    lane = lax.rem(lax.broadcasted_iota(jnp.int32, (1, query_rows), 1), rows)
    query_pos = lane + jnp.where(
        lane < span, pos_ref[PAIR * c] * span, pos_ref[PAIR * c + 1] * span - span
    )
    key_offset = lax.broadcasted_iota(jnp.int32, (span, 1), 0)

    row_max[...] = jnp.full_like(row_max, -jnp.inf)
    row_sum[...] = jnp.zeros_like(row_sum)
    dq_t[...] = jnp.zeros_like(dq_t)

    def score_block(which, group, other):
        raw = nn_dot(kv[0, group, other], q_cols[...]) * (SCORE_SCALE * LOG2_E)
        best = row_max[which]
        for part in range(2):
            key_pos = pos_ref[2 * (other * PAIR + group) + part] * span + key_offset
            masked = jnp.where(key_pos <= query_pos, raw[part * span : (part + 1) * span], -jnp.inf)
            scores[which, other, part * span : (part + 1) * span, :] = masked
            best = jnp.maximum(best, jnp.max(masked, axis=0, keepdims=True))
        row_max[which] = best

    def exp_block(which, other):
        weights = jnp.exp2(scores[which, other] - row_max[which])
        scores[which, other] = weights
        row_sum[which] += jnp.sum(weights, axis=0, keepdims=True)

    def value_block(which, other, factor):
        probs = scores[which, other] * factor
        scores[which, other] = probs
        part = nn_dot(probs.astype(jnp.bfloat16), g_rows[...])
        target = pair_out if which == 1 else own_part
        target[1, other] = part.astype(target.dtype)

    def key_block(which, group, other):
        grad_probs = nn_dot(kv[1, group, other], g_cols[...])
        grads = (scores[which, other] * (grad_probs - delta[...])).astype(jnp.bfloat16)
        grad_scores[which, other] = grads
        part = nn_dot(grads, q_rows[...]) * SCORE_SCALE
        target = pair_out if which == 1 else own_part
        target[0, other] = part.astype(target.dtype)

    def query_chunk(which, group, index):
        at = pl.ds(index * chunk, chunk)
        keys = kv[0, group, at].reshape(chunk_rows, HEAD_SIZE)
        dq_t[...] += tn_dot(keys, grad_scores[which, at].reshape(chunk_rows, query_rows))

    def across(kind):
        return pltpu.make_async_remote_copy(
            src_ref=kv.at[kind, 1 - b, a],
            dst_ref=kv.at[kind, 1 - b, a],
            send_sem=across_send.at[kind],
            recv_sem=kv_recv.at[kind, 1 - b, a],
            device_id=far_device(far(1)),
            device_id_type=MESH,
        )

    def pass_across(kind):
        forward(kind, 1 - b, a).wait_recv()
        across(kind).start()

    def key_arrival(i):
        other = far(i + 2)
        forward(0, b, other).wait_recv()
        forward(0, b, other).start()
        score_block(0, b, other)

    def value_arrival(i):
        other = far(i + 2)
        forward(1, b, other).wait_recv()
        forward(1, b, other).start()

    def pair_key_arrival(i):
        other = far(i + 1)
        forward(0, 1 - b, other).wait_recv()
        score_block(1, 1 - b, other)

    local_copies[3].wait()
    score_block(0, b, a)
    pass_across(0)
    each(far_size - 2, key_arrival)
    forward(0, b, far(1)).wait_recv()
    score_block(0, b, far(1))
    pass_across(1)
    each(far_size - 2, value_arrival)
    forward(1, b, far(1)).wait_recv()
    each(far_size, lambda i: exp_block(0, i))
    score_block(1, 1 - b, a)
    each(far_size - 1, pair_key_arrival)
    row_max[1] = jnp.maximum(row_max[0], row_max[1])
    each(far_size, lambda i: exp_block(1, i))
    own_shrink = jnp.exp2(row_max[0] - row_max[1])
    pair_factor = 1.0 / (row_sum[0] * own_shrink + row_sum[1])
    own_factor = own_shrink * pair_factor
    local_copies[4].wait()

    def pair_copy(kind, other):
        return pltpu.make_async_remote_copy(
            src_ref=pair_out.at[kind, other],
            dst_ref=pair_in.at[kind, other],
            send_sem=pair_send.at[kind, other],
            recv_sem=pair_recv.at[kind, other],
            device_id=partner,
            device_id_type=MESH,
        )

    def far_copy(kind, i):
        return pltpu.make_async_remote_copy(
            src_ref=far_out.at[kind, i],
            dst_ref=far_in.at[kind, i],
            send_sem=far_send.at[kind, i],
            recv_sem=far_recv.at[kind, i],
            device_id=far_device(far(i + 1)),
            device_id_type=MESH,
        )

    def send_far(kind, i):
        other = far(i + 1)
        pair_copy(kind, other).wait_recv()
        far_out[kind, i] = (
            own_part[kind, other] + pair_in[kind, other].astype(jnp.float32)
        ).astype(jnp.bfloat16)
        far_copy(kind, i).start()

    def pair_value(i):
        other = far(lax.rem(i + 1, far_size) if far_size > 8 else (i + 1) % far_size)
        value_block(1, other, pair_factor)
        pair_copy(1, other).start()

    def pair_key(i):
        other = far(i + 1)
        forward(1, 1 - b, other).wait_recv()
        key_block(1, 1 - b, other)
        pair_copy(0, other).start()

    each(far_size, pair_value)
    each(far_size, lambda i: value_block(0, i, own_factor))
    each(far_size - 1, pair_key)
    key_block(1, 1 - b, a)
    pair_copy(0, a).start()
    each(far_size, lambda i: key_block(0, b, i))
    each(far_size - 1, lambda i: send_far(1, i))

    each(chunks, lambda i: query_chunk(1, 1 - b, i))
    each(chunks, lambda i: query_chunk(0, b, i))
    local_copies[5].wait()
    grad_query = (dq_t[...] * SCORE_SCALE).astype(jnp.bfloat16)
    stacked = jnp.concatenate(
        [grad_query[:, head * rows : (head + 1) * rows] for head in range(heads)], axis=0
    )

    def tp_copy(step):
        return pltpu.make_async_remote_copy(
            src_ref=tp_out.at[step - 1],
            dst_ref=tp_in.at[step - 1],
            send_sem=tp_send.at[step - 1],
            recv_sem=tp_recv.at[step - 1],
            device_id=(c, tp_peer(step)),
            device_id_type=MESH,
        )

    for step in order:
        tp_out[step - 1] = nn_dot(wq[feature_rows(tp_peer(step)), :], stacked).astype(jnp.bfloat16)
        tp_copy(step).start()
    each(far_size - 1, lambda i: send_far(0, i))
    own_proj = nn_dot(wq[own_features, :], stacked)

    def grad_copy(step, kind):
        return pltpu.make_async_remote_copy(
            src_ref=g_kv.at[t, kind],
            dst_ref=g_kv.at[t, kind],
            send_sem=g_send.at[step - 1, kind],
            recv_sem=g_recv.at[step - 1, kind],
            device_id=(c, tp_peer(step)),
            device_id_type=MESH,
        )

    def add_far(kind, i):
        far_copy(kind, i).wait_recv()
        own_part[kind, a] += far_in[kind, i].astype(jnp.float32)

    def finish(kind):
        pair_copy(kind, a).wait_recv()
        own_part[kind, a] += pair_in[kind, a].astype(jnp.float32)
        each(far_size - 1, lambda i: add_far(kind, i))
        g_kv[t, kind] = own_part[kind, a].T.astype(jnp.bfloat16)
        for step in order:
            grad_copy(step, kind).start()

    finish(1)
    for step in reversed(order):
        tp_copy(step).wait_recv()
        own_proj += tp_in[step - 1].astype(jnp.float32)
    for kind in range(2):
        each(far_size - 1, lambda i, kind=kind: direct_copy(kind, i).wait_send())
        own_forward(kind).wait_send()
        across(kind).wait_send()
        each(far_size - 2, lambda i, kind=kind: forward(kind, b, far(i + 2)).wait_send())
        each(far_size, lambda i, kind=kind: pair_copy(kind, i).wait_send())
        local_copies[6 + kind].wait()
        for step in order:
            weight_copy(step, kind).wait_recv()
            weight_copy(step, kind).wait_send()
    for step in order:
        tp_copy(step).wait_send()
    finish(0)
    total = own_proj
    for kind in (1, 0):
        total += nn_dot(w_kv[t, kind], g_kv[t, kind])
        for step in reversed(order):
            sender = lax.rem(t + tp_size - step, tp_size)
            grad_copy(step, kind).wait_recv()
            total += nn_dot(w_kv[sender, kind], g_kv[sender, kind])
    out_ref[...] = total.T.astype(out_ref.dtype)

    for kind in range(2):
        each(far_size - 1, lambda i, kind=kind: far_copy(kind, i).wait_send())
        for step in order:
            grad_copy(step, kind).wait_send()


def local(ctx_size, tp_size, queries, key_rows, value_matrix, attention_out, output_grad, w_query, key_weight, value_weight, span_pos):
    rows, width = queries.shape
    model = w_query.shape[0]
    query_rows = rows * (width // HEAD_SIZE)
    far_size = ctx_size // PAIR
    features = model // tp_size
    block = (rows, HEAD_SIZE)
    low, full = jnp.bfloat16, jnp.float32
    dma = pltpu.SemaphoreType.DMA
    in_hbm = pl.BlockSpec(memory_space=pltpu.HBM)
    return pl.pallas_call(
        functools.partial(kernel, ctx_size, tp_size),
        out_shape=pltpu.VMEM((rows, features), low),
        in_specs=[in_hbm] * 8 + [pl.BlockSpec(memory_space=pltpu.SMEM)],
        out_specs=pl.BlockSpec(memory_space=pltpu.VMEM),
        scratch_shapes=[
            pltpu.VMEM((rows, width), low),
            pltpu.VMEM((rows, width), low),
            pltpu.VMEM((rows, width), low),
            pltpu.VMEM(w_query.shape, low),
            pltpu.VMEM((tp_size, 2, features, HEAD_SIZE), low),
            pltpu.VMEM((2, PAIR, far_size) + block, low),
            pltpu.VMEM((query_rows, HEAD_SIZE), low),
            pltpu.VMEM((query_rows, HEAD_SIZE), low),
            pltpu.VMEM((HEAD_SIZE, query_rows), low),
            pltpu.VMEM((HEAD_SIZE, query_rows), low),
            pltpu.VMEM((1, query_rows), full),
            pltpu.VMEM((PAIR, far_size, rows, query_rows), full),
            pltpu.VMEM((PAIR, far_size, rows, query_rows), low),
            pltpu.VMEM((PAIR, 1, query_rows), full),
            pltpu.VMEM((PAIR, 1, query_rows), full),
            pltpu.VMEM((HEAD_SIZE, query_rows), full),
            pltpu.VMEM((2, far_size) + block, low),
            pltpu.VMEM((2, far_size) + block, low),
            pltpu.VMEM((2, far_size) + block, full),
            pltpu.VMEM((2, far_size - 1) + block, low),
            pltpu.VMEM((2, far_size - 1) + block, low),
            pltpu.VMEM((tp_size - 1, features, rows), low),
            pltpu.VMEM((tp_size - 1, features, rows), low),
            dma((8,)),
            dma((2, far_size - 1)),
            dma((2, far_size)),
            dma((2, PAIR, far_size)),
            dma((2, far_size)),
            dma((2, far_size)),
            dma((2, far_size - 1)),
            dma((2, far_size - 1)),
            dma((tp_size - 1,)),
            dma((tp_size - 1,)),
            pltpu.VMEM((tp_size, 2, HEAD_SIZE, rows), low),
            dma((tp_size - 1, 2)),
            dma((tp_size - 1, 2)),
            dma((tp_size - 1, 2)),
            dma((tp_size - 1, 2)),
            dma((2,)),
        ],
        compiler_params=pltpu.CompilerParams(
            collective_id=0, has_side_effects=True, vmem_limit_bytes=(65536 - 192) * 1024
        ),
    )(queries, key_rows, value_matrix, attention_out, output_grad, w_query, key_weight, value_weight, span_pos)


def solution(mesh):
    in_specs = (
        P("ctx", "tp"),
        P("ctx", "tp"),
        P("ctx", "tp"),
        P("ctx", "tp"),
        P("ctx", "tp"),
        P(None, "tp"),
        P(None, "tp"),
        P(None, "tp"),
        P(),
    )
    body = functools.partial(local, mesh.shape["ctx"], mesh.shape["tp"])
    return jax.shard_map(body, mesh=mesh, in_specs=in_specs, out_specs=P("ctx", "tp"), check_vma=False)
```

```python
import functools

import jax
import jax.numpy as jnp
from jax import lax
from jax.experimental import pallas as pl
from jax.experimental.pallas import tpu as pltpu
from jax.sharding import PartitionSpec as P

HEAD_SIZE = 128
PAIR = 2
SCORE_SCALE = HEAD_SIZE ** (-0.5)
LOG2_E = 1.4426950408889634
MESH = pl.DeviceIdType.MESH


def nt_dot(left, right):
    return lax.dot_general(
        left, right, (((1,), (1,)), ((), ())), preferred_element_type=jnp.float32
    )


def nn_dot(left, right):
    return lax.dot_general(
        left, right, (((1,), (0,)), ((), ())), preferred_element_type=jnp.float32
    )


def tn_dot(left, right):
    return lax.dot_general(
        left, right, (((0,), (0,)), ((), ())), preferred_element_type=jnp.float32
    )


def each(count, body):
    if count <= 8:
        for index in range(count):
            body(index)
    else:
        lax.fori_loop(0, count, lambda index, _: (body(index), 0)[1], 0)


def kernel(
    ctx_size,
    tp_size,
    q_ref,
    k_ref,
    v_ref,
    o_ref,
    g_ref,
    wq_ref,
    wk_ref,
    wv_ref,
    pos_ref,
    out_ref,
    q_in,
    g_in,
    o_in,
    wq,
    w_kv,
    kv,
    q_rows,
    g_rows,
    delta,
    scores,
    grad_scores,
    row_max,
    row_sum,
    dq_t,
    pair_out,
    pair_in,
    own_part,
    far_out,
    far_in,
    tp_out,
    tp_in,
    local_sem,
    kv_send,
    kv_fwd,
    kv_recv,
    pair_send,
    pair_recv,
    far_send,
    far_recv,
    tp_send,
    tp_recv,
    g_kv,
    w_send,
    w_recv,
    g_send,
    g_recv,
):
    rows = q_ref.shape[0]
    span = rows // 2
    heads = q_ref.shape[1] // HEAD_SIZE
    query_rows = heads * rows
    far_size = ctx_size // PAIR
    features = out_ref.shape[1]
    chunk = min(far_size, 4)
    chunks = far_size // chunk
    chunk_rows = chunk * rows

    c = lax.axis_index("ctx")
    t = lax.axis_index("tp")
    a = lax.div(c, PAIR)
    b = lax.rem(c, PAIR)
    partner = (a * PAIR + 1 - b, t)

    def far(step):
        return lax.rem(a + step, far_size)

    def far_device(other):
        return (other * PAIR + b, t)

    def feature_rows(owner):
        return pl.ds(pl.multiple_of(owner * features, features), features)

    def tp_peer(step):
        return lax.rem(t + step, tp_size)

    own_features = feature_rows(t)
    order = sorted(range(1, tp_size), key=lambda step: abs(step - tp_size // 2))

    local_pairs = [
        (q_ref, q_in),
        (g_ref, g_in),
        (o_ref, o_in),
        (k_ref, kv.at[0, b, a]),
        (v_ref, kv.at[1, b, a]),
        (wq_ref, wq),
        (wk_ref.at[own_features], w_kv.at[t, 0]),
        (wv_ref.at[own_features], w_kv.at[t, 1]),
    ]
    local_copies = [
        pltpu.make_async_copy(src, dst, local_sem.at[i]) for i, (src, dst) in enumerate(local_pairs)
    ]
    for copy in local_copies:
        copy.start()

    barrier = pltpu.get_barrier_semaphore()

    def greet_far(i):
        pl.semaphore_signal(barrier, inc=1, device_id=far_device(far(i + 1)), device_id_type=MESH)

    each(far_size - 1, greet_far)
    pl.semaphore_signal(barrier, inc=1, device_id=partner, device_id_type=MESH)
    for step in range(1, tp_size):
        pl.semaphore_signal(
            barrier, inc=1, device_id=(c, lax.rem(t + step, tp_size)), device_id_type=MESH
        )
    pl.semaphore_wait(barrier, far_size - 1 + 1 + tp_size - 1)

    def direct_copy(kind, i):
        return pltpu.make_async_remote_copy(
            src_ref=(k_ref, v_ref)[kind],
            dst_ref=kv.at[kind, b, a],
            send_sem=kv_send.at[kind, i],
            recv_sem=kv_recv.at[kind, b, a],
            device_id=far_device(far(i + 1)),
            device_id_type=MESH,
        )

    def own_forward(kind):
        return pltpu.make_async_remote_copy(
            src_ref=(k_ref, v_ref)[kind],
            dst_ref=kv.at[kind, b, a],
            send_sem=kv_fwd.at[kind, a],
            recv_sem=kv_recv.at[kind, b, a],
            device_id=partner,
            device_id_type=MESH,
        )

    def forward(kind, group, other):
        return pltpu.make_async_remote_copy(
            src_ref=kv.at[kind, group, other],
            dst_ref=kv.at[kind, group, other],
            send_sem=kv_fwd.at[kind, other],
            recv_sem=kv_recv.at[kind, group, other],
            device_id=partner,
            device_id_type=MESH,
        )

    for kind in range(2):
        each(far_size - 1, lambda i, kind=kind: direct_copy(kind, i).start())
        own_forward(kind).start()

    def weight_copy(step, kind):
        return pltpu.make_async_remote_copy(
            src_ref=(wk_ref, wv_ref)[kind].at[feature_rows(tp_peer(step))],
            dst_ref=w_kv.at[t, kind],
            send_sem=w_send.at[step - 1, kind],
            recv_sem=w_recv.at[step - 1, kind],
            device_id=(c, tp_peer(step)),
            device_id_type=MESH,
        )

    for copy in local_copies[:3]:
        copy.wait()
    for head in range(heads):
        lanes = slice(head * HEAD_SIZE, (head + 1) * HEAD_SIZE)
        held = slice(head * rows, (head + 1) * rows)
        q_rows[held, :] = q_in[:, lanes]
        g_head = g_in[:, lanes]
        g_rows[held, :] = g_head
        products = g_head.astype(jnp.float32) * o_in[:, lanes].astype(jnp.float32)
        delta[:, held] = jnp.sum(products.T, axis=0, keepdims=True)

    lane = lax.rem(lax.broadcasted_iota(jnp.int32, (1, query_rows), 1), rows)
    query_pos = lane + jnp.where(
        lane < span, pos_ref[PAIR * c] * span, pos_ref[PAIR * c + 1] * span - span
    )
    key_offset = lax.broadcasted_iota(jnp.int32, (span, 1), 0)

    row_max[...] = jnp.full_like(row_max, -jnp.inf)
    row_sum[...] = jnp.zeros_like(row_sum)
    dq_t[...] = jnp.zeros_like(dq_t)

    def score_block(which, group, other):
        raw = nt_dot(kv[0, group, other], q_rows[...]) * (SCORE_SCALE * LOG2_E)
        best = row_max[which]
        for part in range(2):
            key_pos = pos_ref[2 * (other * PAIR + group) + part] * span + key_offset
            masked = jnp.where(key_pos <= query_pos, raw[part * span : (part + 1) * span], -jnp.inf)
            scores[which, other, part * span : (part + 1) * span, :] = masked
            best = jnp.maximum(best, jnp.max(masked, axis=0, keepdims=True))
        row_max[which] = best

    def exp_block(which, other):
        weights = jnp.exp2(scores[which, other] - row_max[which])
        scores[which, other] = weights
        row_sum[which] += jnp.sum(weights, axis=0, keepdims=True)

    def value_block(which, other, factor):
        probs = scores[which, other] * factor
        scores[which, other] = probs
        part = nn_dot(probs.astype(jnp.bfloat16), g_rows[...])
        target = pair_out if which == 1 else own_part
        target[1, other] = part.astype(target.dtype)

    def key_block(which, group, other):
        grad_probs = nt_dot(kv[1, group, other], g_rows[...])
        grads = (scores[which, other] * (grad_probs - delta[...])).astype(jnp.bfloat16)
        grad_scores[which, other] = grads
        part = nn_dot(grads, q_rows[...]) * SCORE_SCALE
        target = pair_out if which == 1 else own_part
        target[0, other] = part.astype(target.dtype)

    def query_chunk(which, group, index):
        at = pl.ds(index * chunk, chunk)
        keys = kv[0, group, at].reshape(chunk_rows, HEAD_SIZE)
        dq_t[...] += tn_dot(keys, grad_scores[which, at].reshape(chunk_rows, query_rows))

    def key_arrival(i):
        other = far(i + 1)
        forward(0, b, other).wait_recv()
        forward(0, b, other).start()
        score_block(0, b, other)

    def value_arrival(i):
        other = far(i + 1)
        forward(1, b, other).wait_recv()
        forward(1, b, other).start()

    def pair_key_arrival(i):
        other = far(i)
        forward(0, 1 - b, other).wait_recv()
        score_block(1, 1 - b, other)

    local_copies[3].wait()
    score_block(0, b, a)
    each(far_size - 1, key_arrival)
    each(far_size - 1, value_arrival)
    for kind in (1, 0):
        for step in order:
            weight_copy(step, kind).start()
    each(far_size, lambda i: exp_block(0, i))
    each(far_size, pair_key_arrival)
    row_max[1] = jnp.maximum(row_max[0], row_max[1])
    each(far_size, lambda i: exp_block(1, i))
    own_shrink = jnp.exp2(row_max[0] - row_max[1])
    pair_factor = 1.0 / (row_sum[0] * own_shrink + row_sum[1])
    own_factor = own_shrink * pair_factor
    local_copies[4].wait()

    def pair_copy(kind, other):
        return pltpu.make_async_remote_copy(
            src_ref=pair_out.at[kind, other],
            dst_ref=pair_in.at[kind, other],
            send_sem=pair_send.at[kind, other],
            recv_sem=pair_recv.at[kind, other],
            device_id=partner,
            device_id_type=MESH,
        )

    def far_copy(kind, i):
        return pltpu.make_async_remote_copy(
            src_ref=far_out.at[kind, i],
            dst_ref=far_in.at[kind, i],
            send_sem=far_send.at[kind, i],
            recv_sem=far_recv.at[kind, i],
            device_id=far_device(far(i + 1)),
            device_id_type=MESH,
        )

    def send_far(kind, i):
        other = far(i + 1)
        pair_copy(kind, other).wait_recv()
        far_out[kind, i] = (
            own_part[kind, other] + pair_in[kind, other].astype(jnp.float32)
        ).astype(jnp.bfloat16)
        far_copy(kind, i).start()

    def pair_value(i):
        other = far(i + 1)
        value_block(1, other, pair_factor)
        pair_copy(1, other).start()

    def pair_key(i):
        other = far(i + 1)
        forward(1, 1 - b, other).wait_recv()
        key_block(1, 1 - b, other)
        pair_copy(0, other).start()

    each(far_size, pair_value)
    each(far_size, lambda i: value_block(0, i, own_factor))
    each(far_size, pair_key)
    each(far_size, lambda i: key_block(0, b, i))
    each(far_size - 1, lambda i: send_far(1, i))

    each(chunks, lambda i: query_chunk(1, 1 - b, i))
    each(chunks, lambda i: query_chunk(0, b, i))
    local_copies[5].wait()
    grad_query = (dq_t[...] * SCORE_SCALE).astype(jnp.bfloat16)
    stacked = jnp.concatenate(
        [grad_query[:, head * rows : (head + 1) * rows] for head in range(heads)], axis=0
    )

    def tp_copy(step):
        return pltpu.make_async_remote_copy(
            src_ref=tp_out.at[step - 1],
            dst_ref=tp_in.at[step - 1],
            send_sem=tp_send.at[step - 1],
            recv_sem=tp_recv.at[step - 1],
            device_id=(c, tp_peer(step)),
            device_id_type=MESH,
        )

    for step in order:
        tp_out[step - 1] = nn_dot(wq[feature_rows(tp_peer(step)), :], stacked).astype(jnp.bfloat16)
        tp_copy(step).start()
    each(far_size - 1, lambda i: send_far(0, i))
    own_proj = nn_dot(wq[own_features, :], stacked)

    def grad_copy(step, kind):
        return pltpu.make_async_remote_copy(
            src_ref=g_kv.at[t, kind],
            dst_ref=g_kv.at[t, kind],
            send_sem=g_send.at[step - 1, kind],
            recv_sem=g_recv.at[step - 1, kind],
            device_id=(c, tp_peer(step)),
            device_id_type=MESH,
        )

    def add_far(kind, i):
        far_copy(kind, i).wait_recv()
        own_part[kind, a] += far_in[kind, i].astype(jnp.float32)

    def finish(kind):
        pair_copy(kind, a).wait_recv()
        own_part[kind, a] += pair_in[kind, a].astype(jnp.float32)
        each(far_size - 1, lambda i: add_far(kind, i))
        g_kv[t, kind] = own_part[kind, a].astype(jnp.bfloat16)
        for step in order:
            grad_copy(step, kind).start()

    finish(1)
    for step in reversed(order):
        tp_copy(step).wait_recv()
        own_proj += tp_in[step - 1].astype(jnp.float32)
    total = own_proj.T
    finish(0)
    for kind in (1, 0):
        local_copies[6 + kind].wait()
        total += nt_dot(g_kv[t, kind], w_kv[t, kind])
        for step in reversed(order):
            sender = lax.rem(t + tp_size - step, tp_size)
            weight_copy(step, kind).wait_recv()
            grad_copy(step, kind).wait_recv()
            total += nt_dot(g_kv[sender, kind], w_kv[sender, kind])
    out_ref[...] = total.astype(out_ref.dtype)

    for kind in range(2):
        each(far_size - 1, lambda i, kind=kind: direct_copy(kind, i).wait_send())
        each(far_size, lambda i, kind=kind: forward(kind, b, i).wait_send())
        each(far_size, lambda i, kind=kind: pair_copy(kind, i).wait_send())
        each(far_size - 1, lambda i, kind=kind: far_copy(kind, i).wait_send())
        for step in order:
            weight_copy(step, kind).wait_send()
            grad_copy(step, kind).wait_send()
    for step in order:
        tp_copy(step).wait_send()


def local(ctx_size, tp_size, queries, key_rows, value_matrix, attention_out, output_grad, w_query, key_weight, value_weight, span_pos):
    rows, width = queries.shape
    model = w_query.shape[0]
    query_rows = rows * (width // HEAD_SIZE)
    far_size = ctx_size // PAIR
    features = model // tp_size
    block = (rows, HEAD_SIZE)
    low, full = jnp.bfloat16, jnp.float32
    dma = pltpu.SemaphoreType.DMA
    in_hbm = pl.BlockSpec(memory_space=pltpu.HBM)
    return pl.pallas_call(
        functools.partial(kernel, ctx_size, tp_size),
        out_shape=pltpu.VMEM((rows, features), low),
        in_specs=[in_hbm] * 8 + [pl.BlockSpec(memory_space=pltpu.SMEM)],
        out_specs=pl.BlockSpec(memory_space=pltpu.VMEM),
        scratch_shapes=[
            pltpu.VMEM((rows, width), low),
            pltpu.VMEM((rows, width), low),
            pltpu.VMEM((rows, width), low),
            pltpu.VMEM(w_query.shape, low),
            pltpu.VMEM((tp_size, 2, features, HEAD_SIZE), low),
            pltpu.VMEM((2, PAIR, far_size) + block, low),
            pltpu.VMEM((query_rows, HEAD_SIZE), low),
            pltpu.VMEM((query_rows, HEAD_SIZE), low),
            pltpu.VMEM((1, query_rows), full),
            pltpu.VMEM((PAIR, far_size, rows, query_rows), full),
            pltpu.VMEM((PAIR, far_size, rows, query_rows), low),
            pltpu.VMEM((PAIR, 1, query_rows), full),
            pltpu.VMEM((PAIR, 1, query_rows), full),
            pltpu.VMEM((HEAD_SIZE, query_rows), full),
            pltpu.VMEM((2, far_size) + block, low),
            pltpu.VMEM((2, far_size) + block, low),
            pltpu.VMEM((2, far_size) + block, full),
            pltpu.VMEM((2, far_size - 1) + block, low),
            pltpu.VMEM((2, far_size - 1) + block, low),
            pltpu.VMEM((tp_size - 1, features, rows), low),
            pltpu.VMEM((tp_size - 1, features, rows), low),
            dma((8,)),
            dma((2, far_size - 1)),
            dma((2, far_size)),
            dma((2, PAIR, far_size)),
            dma((2, far_size)),
            dma((2, far_size)),
            dma((2, far_size - 1)),
            dma((2, far_size - 1)),
            dma((tp_size - 1,)),
            dma((tp_size - 1,)),
            pltpu.VMEM((tp_size, 2) + block, low),
            dma((tp_size - 1, 2)),
            dma((tp_size - 1, 2)),
            dma((tp_size - 1, 2)),
            dma((tp_size - 1, 2)),
        ],
        compiler_params=pltpu.CompilerParams(
            collective_id=0, has_side_effects=True, vmem_limit_bytes=(65536 - 192) * 1024
        ),
    )(queries, key_rows, value_matrix, attention_out, output_grad, w_query, key_weight, value_weight, span_pos)


def solution(mesh):
    in_specs = (
        P("ctx", "tp"),
        P("ctx", "tp"),
        P("ctx", "tp"),
        P("ctx", "tp"),
        P("ctx", "tp"),
        P(None, "tp"),
        P(None, "tp"),
        P(None, "tp"),
        P(),
    )
    body = functools.partial(local, mesh.shape["ctx"], mesh.shape["tp"])
    return jax.shard_map(body, mesh=mesh, in_specs=in_specs, out_specs=P("ctx", "tp"), check_vma=False)
```
